32 devices in a mesh: tm: 8 (over y, x, core), tile: 4 (over z).
Axes of the slice: x: 2, y: 2, z: 4, core: 2. Of those that a mesh axis runs over, the one named last changes fastest.
Arguments:
- latent: bfloat16 [16, 16, 128, 16], P('tm', 'tile'), may hold values from -6 to 6
- cache_lat: bfloat16 [2, 16, 128, 16], P(None, 'tile'), may hold values from -6 to 6
- cache_one: bfloat16 [2, 16, 128, 384], P(None, 'tile'), may hold values from -6 to 6
- cache_two: bfloat16 [2, 16, 128, 384], P(None, 'tile'), may hold values from -6 to 6
- w_in: bfloat16 [3, 3, 3, 16, 384], replicated, may hold values from -0.3125 to 0.3125
- b_in: float32 [384], replicated, may hold values from -3 to 3
- gain_one: float32 [384], replicated, may hold values from 0.1 to 1.9
- w_one: bfloat16 [3, 3, 3, 384, 384], replicated, may hold values from -0.0625 to 0.0625
- b_one: float32 [384], replicated, may hold values from -3 to 3
- gain_two: float32 [384], replicated, may hold values from 0.1 to 1.9
- w_two: bfloat16 [3, 3, 3, 384, 384], replicated, may hold values from -0.0625 to 0.0625
- b_two: float32 [384], replicated, may hold values from -3 to 3
Outputs:
- decoded: bfloat16 [16, 16, 128, 384], P('tm', 'tile')
The draws below stay inside these ranges and needn't reach their ends.
All inputs are finite; a program needn't handle non-finite values.
Results may differ from the reference program's by a relative error of at most 0.0051.
Values may be sent and summed in bfloat16 or wider, within the bound.
No kernel may reach another device: no remote copies, remote signals or barrier semaphores. Data moves between devices by JAX's collectives and lax.ppermute only.
A program may use at most 320 MiB of HBM per device.

```python
import jax
import jax.numpy as jnp
from jax import lax

CIN = 16
C = 384
WIDE = 128
TT = 16
HH = 16


def levels(rng, shape, split, least, largest):
    loudness, own = 1.0, jax.random.fold_in(rng, 6)
    for dim, parts in split:
        draws = jnp.exp(jax.random.uniform(jax.random.fold_in(own, dim), (parts,), jnp.float32, least / len(split), largest / len(split)))
        loudness = loudness * jnp.repeat(draws, shape[dim] // parts).reshape([-1 if axis == dim else 1 for axis in range(len(shape))])
    return loudness


def scatter_about(own_key, shape, scale, most, shards=(), held_as=jnp.bfloat16):
    drawn = scale * jax.random.normal(own_key, shape, jnp.float32)
    if shards:
        drawn = drawn * levels(own_key, shape, shards, -0.22, 0.18)
    return jnp.clip(drawn, -most, most).astype(held_as)


def setup_inputs(seed: int = 0) -> dict:
    arg_keys = jax.random.split(jax.random.key(seed), 13)
    latent = scatter_about(arg_keys[0], (TT, HH, WIDE, CIN), 1.0, 6.0, ((0, 8), (1, 4)))
    cache_lat = scatter_about(arg_keys[1], (2, HH, WIDE, CIN), 1.0, 6.0, ((1, 4),))
    cache_one = scatter_about(arg_keys[2], (2, HH, WIDE, C), 1.0, 6.0, ((1, 4),))
    cache_two = scatter_about(arg_keys[3], (2, HH, WIDE, C), 1.0, 6.0, ((1, 4),))
    w_in = scatter_about(arg_keys[4], (3, 3, 3, CIN, C), (27 * CIN) ** -0.5, 0.3125)
    b_in = scatter_about(arg_keys[5], (C,), 0.5, 3.0, (), jnp.float32)
    gain_one = jnp.clip(1.0 + 0.18 * jax.random.normal(arg_keys[6], (C,), jnp.float32), 0.1, 1.9)
    w_one = scatter_about(arg_keys[7], (3, 3, 3, C, C), (27 * C) ** -0.5, 0.0625)
    b_one = scatter_about(arg_keys[8], (C,), 0.5, 3.0, (), jnp.float32)
    gain_two = jnp.clip(1.0 + 0.18 * jax.random.normal(arg_keys[9], (C,), jnp.float32), 0.1, 1.9)
    w_two = scatter_about(arg_keys[10], (3, 3, 3, C, C), (27 * C) ** -0.5, 0.0625)
    b_two = scatter_about(arg_keys[11], (C,), 0.5, 3.0, (), jnp.float32)
    return {"latent": latent, "cache_lat": cache_lat, "cache_one": cache_one, "cache_two": cache_two, "w_in": w_in, "b_in": b_in, "gain_one": gain_one, "w_one": w_one, "b_one": b_one, "gain_two": gain_two, "w_two": w_two, "b_two": b_two}


def conv_full(values, cache, kernel, bias):
    frames, height, width, chan = values.shape
    outc = kernel.shape[-1]
    full = jnp.concatenate([cache, values], 0)
    full = jnp.pad(full, ((0, 0), (1, 1), (1, 1), (0, 0)))
    total = jnp.zeros((frames * height * width, outc), jnp.float32)
    for dt in range(3):
        for dy in range(3):
            for dx in range(3):
                window = full[dt:dt + frames, dy:dy + height, dx:dx + width].reshape(-1, chan)
                total = total + jnp.dot(window, kernel[dt, dy, dx], preferred_element_type=jnp.float32)
    return total.reshape(frames, height, width, outc) + bias

def rms_norm(values, gain):
    return values * jax.lax.rsqrt(lax.optimization_barrier(jnp.mean(values * values, -1, keepdims=True)) + 1e-06) * gain

def reference(latent, cache_lat, cache_one, cache_two, w_in, b_in, gain_one, w_one, b_one, gain_two, w_two, b_two):
    first = conv_full(latent, cache_lat, w_in, b_in).astype(jnp.bfloat16)
    normed = jax.nn.silu(rms_norm(first.astype(jnp.float32), gain_one)).astype(jnp.bfloat16)
    middle = conv_full(normed, cache_one, w_one, b_one)
    normed_two = jax.nn.silu(rms_norm(middle, gain_two)).astype(jnp.bfloat16)
    last = conv_full(normed_two, cache_two, w_two, b_two)
    return (first.astype(jnp.float32) + last).astype(jnp.bfloat16)
```

```python
import functools

import jax
import jax.numpy as jnp
from jax import lax
from jax.experimental import pallas as pl
from jax.experimental.pallas import tpu as pltpu
from jax.sharding import PartitionSpec as P

BF = jnp.bfloat16
F32 = jnp.float32
VMEM = pltpu.VMEM


def shifted(x, axis, by):
    count = lax.axis_size(axis)
    return lax.ppermute(x, axis, [(i, i + by) for i in range(count) if 0 <= i + by < count])


def first_frames_only(x, by):
    rows = lax.axis_size("tile")
    return lax.ppermute(
        x, ("tm", "tile"), [(i, i + by) for i in range(rows) if 0 <= i + by < rows]
    )


def column_of(place, width):
    half = width // 2
    return jnp.where(place < half, 2 * place, 2 * (place - half) + 1)


def silu(v):
    return 0.5 * v * (1.0 + jnp.tanh(0.5 * v))


def rms(v, gain):
    return v * lax.rsqrt(jnp.mean(v * v, -1, keepdims=True) + 1e-6) * gain


def filtered(even, odd):
    half = even.shape[0]
    place = lax.broadcasted_iota(jnp.int32, even.shape, 0)
    odd_before = jnp.where(place == 0, 0.0, pltpu.roll(odd, 1, 0))
    even_after = jnp.where(place == half - 1, 0.0, pltpu.roll(even, half - 1, 0))
    return (
        (odd_before - odd).astype(BF),
        (even + odd).astype(BF),
        (odd - even).astype(BF),
        (even - even_after).astype(BF),
    )


def kernel_sums(w_ref, u_ref):
    g0 = w_ref[0, 0].astype(F32)
    g1 = w_ref[0, 1].astype(F32)
    g2 = w_ref[0, 2].astype(F32)
    s = 0.5 * (g0 + g2)
    h = 0.5 * g1
    u_ref[0, 0] = (s + h).astype(BF)
    u_ref[1, 0] = (s - h).astype(BF)


def summed_kernels(w):
    c, o = w.shape[-2:]
    return pl.pallas_call(
        kernel_sums,
        grid=(9,),
        in_specs=[pl.BlockSpec((1, 3, c, o), lambda i: (i, 0, 0, 0))],
        out_specs=pl.BlockSpec((2, 1, c, o), lambda i: (0, i, 0, 0)),
        out_shape=jax.ShapeDtypeStruct((2, 9, c, o), BF),
        name="kernel_sums",
        cost_estimate=pl.CostEstimate(flops=6 * 9 * c * o, bytes_accessed=10 * 9 * c * o, transcendentals=0),
    )(w.reshape(9, 3, c, o))


def weight_copies(w_hbm, u_hbm, w_v, sems, dts):
    out = []
    for j in range(4):
        row = []
        for dt in dts:
            taps = pl.ds(3 * dt, 3)
            if j == 0:
                src = w_hbm.at[taps, 0]
            elif j == 3:
                src = w_hbm.at[taps, 2]
            else:
                src = u_hbm.at[j - 1, taps]
            row.append(pltpu.make_async_copy(src, w_v.at[j, taps], sems.at[j, dt]))
        out.append(row)
    return out


def taps_of(w_v, j, dt):
    return jnp.concatenate([w_v[j, 3 * dt + dy] for dy in range(3)], 0)


def both(w_v, j, dt_a, dt_b):
    return jnp.concatenate([taps_of(w_v, j, dt_a), taps_of(w_v, j, dt_b)], 1)


def rows_of(v, f, j, rows):
    half, c = v.shape[-2:]
    return jnp.concatenate(
        [v[f, j, dy : dy + rows].reshape(rows * half, c) for dy in range(3)], 1
    )


def dot(a, b):
    return jnp.dot(a, b, preferred_element_type=F32)


def first_conv_body(
    tiles,
    own, prev1, prev2, cache_lat, cache_one, cache_up, cache_dn,
    w_in, b_in, gain_one, w_hbm, u_hbm, b_one, gain_two,
    n2_ref, h0_ref,
    lats, v, w_v, acc, sems,
):
    tm = lax.axis_index("tm")
    tile = lax.axis_index("tile")
    width = own.shape[-1]
    half = width // 2
    chan = w_in.shape[0] // 27
    lat_rows = own.shape[0] // (2 * chan)
    rows1 = lat_rows - 2
    rows2 = rows1 - 2
    rows = rows2 - 2
    c = w_in.shape[1]
    copies = weight_copies(w_hbm, u_hbm, w_v, sems, (0, 1, 2))
    for row in copies:
        for copy in row:
            copy.start()

    to = column_of(lax.broadcasted_iota(jnp.int32, (width, width), 1), width)
    at = lax.broadcasted_iota(jnp.int32, (width, width), 0)
    frame = 2 * lat_rows * chan
    for dx in range(3):
        place = jnp.where(at == to + (dx - 1), 1.0, 0.0).astype(BF)
        two = jnp.where(tm == 1, cache_lat[...], prev2[...])
        one = jnp.where(tm == 0, cache_lat[...], prev1[...])
        lats[dx, 0:frame] = dot(two, place).astype(BF)
        lats[dx, frame : 2 * frame] = dot(one, place).astype(BF)
        lats[dx, 2 * frame : 3 * frame] = dot(own[...], place).astype(BF)

    def valid(r, margin):
        at_row = tile * rows + r - margin
        return jnp.logical_and(at_row >= 0, at_row < tiles * rows)

    def put(f, r, n1):
        parts = filtered(n1[:half], n1[half:])
        for j in range(4):
            v[f, j, r] = parts[j]

    def normed(i, _):
        f = i // (rows1 // 2)
        r0 = 2 * (i % (rows1 // 2))
        patches = []
        for k in range(2):
            pieces = []
            for dt in range(3):
                for dy in range(3):
                    start = pl.multiple_of(((f + dt) * lat_rows + r0 + k + dy) * chan, chan)
                    for dx in range(3):
                        pieces.append(lats[dx, pl.ds(start, chan)])
            patches.append(jnp.concatenate(pieces, 0))
        patches = jnp.concatenate(patches, 1)
        h0 = lax.dot_general(
            patches, w_in[...], (((0,), (0,)), ((), ())), preferred_element_type=F32
        )
        h0 = (h0 + b_in[...]).astype(BF)
        own_rows = jnp.logical_and(f >= 2, jnp.logical_and(r0 >= 2, r0 < 2 + rows))

        @pl.when(own_rows)
        def _():
            for k in range(2):
                h0_ref[f - 2, r0 - 2 + k] = h0[k * width : (k + 1) * width]

        n1 = silu(rms(h0.astype(F32), gain_one[...])).astype(BF).astype(F32)
        for k in range(2):
            here = jnp.where(valid(r0 + k, 2), n1[k * width : (k + 1) * width], 0.0)
            put(f, r0 + k, here)
        return 0

    lax.fori_loop(jnp.where(tm == 0, rows1, 0), 2 * rows1, normed, 0)

    @pl.when(tm == 0)
    def _():
        to = column_of(lax.broadcasted_iota(jnp.int32, (width, width), 0), width)
        at = lax.broadcasted_iota(jnp.int32, (width, width), 1)
        place = jnp.where(at == to, 1.0, 0.0).astype(BF)
        for f in range(2):
            for r in range(rows1):
                if r < 2:
                    row = cache_up[f, r]
                elif r < 2 + rows:
                    row = cache_one[f, r - 2]
                else:
                    row = cache_dn[f, r - 2 - rows]
                put(f, r, dot(place, row))

    for j in range(4):
        for copy in copies[j]:
            copy.wait()
        pair = dot(
            jnp.concatenate([rows_of(v, 1, j, rows2), rows_of(v, 2, j, rows2)], 1),
            jnp.concatenate([both(w_v, j, 1, 0), both(w_v, j, 2, 1)], 0),
        )
        acc[j, 0] = pair[:, :c] + dot(rows_of(v, 0, j, rows2), taps_of(w_v, j, 0))
        acc[j, 1] = pair[:, c:] + dot(rows_of(v, 3, j, rows2), taps_of(w_v, j, 2))

    def finish(i, _):
        t = i // rows2
        r = i % rows2
        m = [acc[j, t, pl.ds(pl.multiple_of(r * half, half), half)] for j in range(4)]
        even = m[0] + m[1] + m[2] + b_one[...]
        odd = m[1] - m[2] - m[3] + b_one[...]
        keep = valid(r, 1)
        for k, part in enumerate((even, odd)):
            n2 = silu(rms(part, gain_two[...]))
            n2_ref[t, r, k * half : (k + 1) * half] = jnp.where(keep, n2, 0.0).astype(BF)
        return 0

    lax.fori_loop(0, 2 * rows2, finish, 0)


def own_frames_body(n2, w_hbm, u_hbm, acc_ref, v, w_v, sems):
    rows2, width, c = n2.shape[1:]
    half = width // 2
    rows = rows2 - 2
    copies = weight_copies(w_hbm, u_hbm, w_v, sems, (1, 2))
    for row in copies:
        for copy in row:
            copy.start()

    def split(i, _):
        f = i // rows2
        r = i % rows2
        row = n2[f, r].astype(F32)
        parts = filtered(row[:half], row[half:])
        for j in range(4):
            v[f, j, r] = parts[j]
        return 0

    lax.fori_loop(0, 2 * rows2, split, 0)
    for j in range(4):
        for copy in copies[j]:
            copy.wait()
        pair = dot(rows_of(v, 0, j, rows), both(w_v, j, 2, 1))
        acc_ref[j, 0] = pair[:, :c]
        acc_ref[j, 1] = pair[:, c:] + dot(rows_of(v, 1, j, rows), taps_of(w_v, j, 2))


def earlier_frames_body(
    earlier, cache_two, cache_up, cache_dn, w_hbm, u_hbm, acc_in, h0, b_two,
    out_ref, v, w_v, acc, sems,
):
    tm = lax.axis_index("tm")
    rows2, width, c = earlier.shape[1:]
    half = width // 2
    rows = rows2 - 2
    copies = weight_copies(w_hbm, u_hbm, w_v, sems, (0, 1))
    for row in copies:
        for copy in row:
            copy.start()

    def put(f, r, row):
        parts = filtered(row[:half], row[half:])
        for j in range(4):
            v[f, j, r] = parts[j]

    @pl.when(tm > 0)
    def _():
        def split(i, _):
            f = i // rows2
            r = i % rows2
            put(f, r, earlier[f, r].astype(F32))
            return 0

        lax.fori_loop(0, 2 * rows2, split, 0)

    @pl.when(tm == 0)
    def _():
        to = column_of(lax.broadcasted_iota(jnp.int32, (width, width), 0), width)
        at = lax.broadcasted_iota(jnp.int32, (width, width), 1)
        place = jnp.where(at == to, 1.0, 0.0).astype(BF)
        for f in range(2):
            for r in range(rows2):
                if r < 1:
                    row = cache_up[f, 2]
                elif r < 1 + rows:
                    row = cache_two[f, r - 1]
                else:
                    row = cache_dn[f, 2]
                put(f, r, dot(place, row))

    for j in range(4):
        for copy in copies[j]:
            copy.wait()
        pair = dot(rows_of(v, 1, j, rows), both(w_v, j, 1, 0))
        acc[j, 0] = acc_in[j, 0] + pair[:, :c] + dot(rows_of(v, 0, j, rows), taps_of(w_v, j, 0))
        acc[j, 1] = acc_in[j, 1] + pair[:, c:]

    frm = lax.broadcasted_iota(jnp.int32, (width, width), 0)
    at = column_of(lax.broadcasted_iota(jnp.int32, (width, width), 1), width)
    back = jnp.where(at == frm, 1.0, 0.0).astype(BF)

    def finish(i, _):
        t = i // rows
        r = i % rows
        m = [acc[j, t, pl.ds(pl.multiple_of(r * half, half), half)] for j in range(4)]
        even = m[0] + m[1] + m[2] + b_two[...]
        odd = m[1] - m[2] - m[3] + b_two[...]
        both_cols = jnp.concatenate([even, odd], 0) + h0[t, r].astype(F32)
        out_ref[t, r] = dot(back, both_cols.astype(BF)).astype(BF)
        return 0

    lax.fori_loop(0, 2 * rows, finish, 0)


def in_vmem(count):
    return [pl.BlockSpec(memory_space=VMEM)] * count


IN_HBM = [pl.BlockSpec(memory_space=pl.ANY)]


def on_device(
    latent, cache_lat, cache_one, cache_two, w_in, b_in, gain_one, w_one, b_one, gain_two, w_two, b_two
):
    tiles = lax.axis_size("tile")
    frames, rows, width, chan = latent.shape
    c = w_in.shape[-1]
    half = width // 2
    params = pltpu.CompilerParams(vmem_limit_bytes=48 << 20)

    lat = jnp.concatenate([jnp.swapaxes(latent, 2, 3), jnp.swapaxes(cache_lat, 2, 3)], 0)
    from_up = shifted(lat[:, rows - 3 :], "tile", 1)
    from_dn = shifted(lat[:, :3], "tile", -1)
    caches = jnp.concatenate([cache_one[:, rows - 2 :], cache_two[:, rows - 1 :]], 1)
    cache_up = first_frames_only(caches, 1)
    caches = jnp.concatenate([cache_one[:, :2], cache_two[:, :1]], 1)
    cache_dn = first_frames_only(caches, -1)
    u_one = summed_kernels(w_one)
    lat = jnp.concatenate([from_up, lat, from_dn], 1)
    own = lat[:frames].reshape(-1, width)
    prev1 = shifted(own, "tm", 1)
    prev2 = shifted(own, "tm", 2)
    u_two = summed_kernels(w_two)
    w1 = w_one.reshape(9, 3, c, c)
    w2 = w_two.reshape(9, 3, c, c)

    def row(x):
        return x.reshape(1, c)

    n2, h0 = pl.pallas_call(
        functools.partial(first_conv_body, tiles),
        out_shape=[
            jax.ShapeDtypeStruct((2, rows + 2, width, c), BF),
            jax.ShapeDtypeStruct((2, rows, width, c), BF),
        ],
        in_specs=in_vmem(10) + IN_HBM * 2 + in_vmem(2),
        out_specs=in_vmem(2),
        scratch_shapes=[
            VMEM((3, 6 * (rows + 6) * chan, width), BF),
            VMEM((4, 4, rows + 4, half, c), BF),
            VMEM((4, 9, c, c), BF),
            VMEM((4, 2, (rows + 2) * half, c), F32),
            pltpu.SemaphoreType.DMA((4, 3)),
        ],
        compiler_params=params,
        name="first_conv",
        cost_estimate=pl.CostEstimate(flops=14_000_000_000, bytes_accessed=14_000_000, transcendentals=0),
    )(
        own, prev1, prev2, lat[frames:].reshape(-1, width), cache_one, cache_up, cache_dn,
        w_in.reshape(-1, c), row(b_in), row(gain_one), w1, u_one, row(b_one), row(gain_two),
    )
    earlier = shifted(n2, "tm", 1)
    acc = pl.pallas_call(
        own_frames_body,
        out_shape=jax.ShapeDtypeStruct((4, 2, rows * half, c), F32),
        in_specs=in_vmem(1) + IN_HBM * 2,
        out_specs=pl.BlockSpec(memory_space=VMEM),
        scratch_shapes=[
            VMEM((2, 4, rows + 2, half, c), BF),
            VMEM((4, 9, c, c), BF),
            pltpu.SemaphoreType.DMA((4, 3)),
        ],
        compiler_params=params,
        name="own_frames",
        cost_estimate=pl.CostEstimate(flops=4_000_000_000, bytes_accessed=14_000_000, transcendentals=0),
    )(n2, w2, u_two)
    return pl.pallas_call(
        earlier_frames_body,
        out_shape=jax.ShapeDtypeStruct((2, rows, width, c), BF),
        in_specs=in_vmem(4) + IN_HBM * 2 + in_vmem(3),
        out_specs=pl.BlockSpec(memory_space=VMEM),
        scratch_shapes=[
            VMEM((2, 4, rows + 2, half, c), BF),
            VMEM((4, 9, c, c), BF),
            VMEM((4, 2, rows * half, c), F32),
            pltpu.SemaphoreType.DMA((4, 3)),
        ],
        compiler_params=params,
        name="earlier_frames",
        cost_estimate=pl.CostEstimate(flops=4_000_000_000, bytes_accessed=14_000_000, transcendentals=0),
    )(earlier, cache_two, cache_up, cache_dn, w2, u_two, acc, h0, row(b_two))


def solution(mesh):
    return jax.shard_map(
        on_device,
        mesh=mesh,
        in_specs=(
            P("tm", "tile", None, None),
            P(None, "tile", None, None),
            P(None, "tile", None, None),
            P(None, "tile", None, None),
            P(),
            P(),
            P(),
            P(),
            P(),
            P(),
            P(),
            P(),
        ),
        out_specs=P("tm", "tile", None, None),
        check_vma=False,
    )
```

```python
import functools

import jax
import jax.numpy as jnp
from jax import lax
from jax.experimental import pallas as pl
from jax.experimental.pallas import tpu as pltpu
from jax.sharding import PartitionSpec as P

BF = jnp.bfloat16
F32 = jnp.float32
VMEM = pltpu.VMEM


def shifted(x, axis, by):
    count = lax.axis_size(axis)
    return lax.ppermute(x, axis, [(i, i + by) for i in range(count) if 0 <= i + by < count])


def first_frames_only(x, by):
    rows = lax.axis_size("tile")
    return lax.ppermute(
        x, ("tm", "tile"), [(i, i + by) for i in range(rows) if 0 <= i + by < rows]
    )


def column_of(place, width):
    half = width // 2
    return jnp.where(place < half, 2 * place, 2 * (place - half) + 1)


def silu(v):
    return 0.5 * v * (1.0 + jnp.tanh(0.5 * v))


def rms(v, gain):
    return v * lax.rsqrt(jnp.mean(v * v, -1, keepdims=True) + 1e-6) * gain


def filtered(even, odd):
    half = even.shape[0]
    place = lax.broadcasted_iota(jnp.int32, even.shape, 0)
    odd_before = jnp.where(place == 0, 0.0, pltpu.roll(odd, 1, 0))
    even_after = jnp.where(place == half - 1, 0.0, pltpu.roll(even, half - 1, 0))
    return (
        (odd_before - odd).astype(BF),
        (even + odd).astype(BF),
        (odd - even).astype(BF),
        (even - even_after).astype(BF),
    )


def summed_kernels_body(w, u):
    def tap(i, _):
        g0 = w[i, 0].astype(F32)
        g1 = w[i, 1].astype(F32)
        g2 = w[i, 2].astype(F32)
        s = 0.5 * (g0 + g2)
        h = 0.5 * g1
        u[0, i] = (s + h).astype(BF)
        u[1, i] = (s - h).astype(BF)
        return 0

    lax.fori_loop(0, w.shape[0], tap, 0)


def summed_kernels(w):
    taps, _, c, o = w.shape
    return pl.pallas_call(
        summed_kernels_body,
        in_specs=in_vmem(1),
        out_specs=in_vmem(1)[0],
        out_shape=jax.ShapeDtypeStruct((2, taps, c, o), BF),
        compiler_params=limit(16),
        name="summed_kernels",
        cost_estimate=pl.CostEstimate(flops=6 * taps * c * o, bytes_accessed=10 * taps * c * o, transcendentals=0),
    )(w)


def taps_of(w, u, j, dt):
    if j == 0 or j == 3:
        parts = [w[3 * dt + dy, 0 if j == 0 else 2] for dy in range(3)]
    else:
        parts = [u[j - 1, 3 * dt + dy] for dy in range(3)]
    return jnp.concatenate(parts, 0)


def both(w, u, j, dt_a, dt_b):
    return jnp.concatenate([taps_of(w, u, j, dt_a), taps_of(w, u, j, dt_b)], 1)


def rows_of(v, f, j, rows):
    half, c = v.shape[-2:]
    return jnp.concatenate(
        [v[f, j, dy : dy + rows].reshape(rows * half, c) for dy in range(3)], 1
    )


def dot(a, b):
    return jnp.dot(a, b, preferred_element_type=F32)


def in_vmem(count):
    return [pl.BlockSpec(memory_space=VMEM)] * count


def limit(mib):
    return pltpu.CompilerParams(vmem_limit_bytes=mib << 20)


def places(width, dx, transposed):
    shape = (width, width)
    to = column_of(lax.broadcasted_iota(jnp.int32, shape, 0 if transposed else 1), width)
    at = lax.broadcasted_iota(jnp.int32, shape, 1 if transposed else 0)
    return jnp.where(at == to + (dx - 1), 1.0, 0.0).astype(BF)


def put(v, f, r, row):
    half = row.shape[0] // 2
    parts = filtered(row[:half], row[half:])
    for j in range(4):
        v[f, j, r] = parts[j]


def first_conv_body(
    tiles,
    own, prev1, prev2, up, dn, cache_one, cache_up, cache_dn,
    w_in, b_in, gain_one, w, u, b_one, gain_two,
    n2_ref, h0_ref,
    lats, g, w_big, hs, v, acc,
):
    tm = lax.axis_index("tm")
    tile = lax.axis_index("tile")
    width = own.shape[-1]
    half = width // 2
    c = w_in.shape[1]
    chan = w_in.shape[0] // 27
    rows = own.shape[0] // (2 * chan)
    lat_rows = rows + 6
    rows1 = rows + 4
    rows2 = rows + 2
    slot = 4 * chan

    lats[...] = jnp.zeros_like(lats)
    place = jnp.concatenate([places(width, dx, False) for dx in range(3)], 1)

    def lay(block, f0, r0, count):
        moved = dot(block, place).astype(BF)
        for i in range(block.shape[0] // chan):
            f, r = f0 + i // count, r0 + i % count
            for dx in range(3):
                lats[f, r * slot + dx * chan : r * slot + (dx + 1) * chan] = moved[
                    i * chan : (i + 1) * chan, dx * width : (dx + 1) * width
                ]

    lay(up[...], 0, 0, 3)
    lay(prev2[...], 0, 3, rows)
    lay(prev1[...], 2, 3, rows)
    lay(own[...], 4, 3, rows)
    lay(dn[...], 0, 3 + rows, 3)
    eye = jnp.where(
        lax.broadcasted_iota(jnp.int32, (width, width), 0)
        == lax.broadcasted_iota(jnp.int32, (width, width), 1),
        1.0,
        0.0,
    ).astype(BF)
    for f in range(6):
        g[f * width : (f + 1) * width] = lax.dot_general(
            eye, lats[f], (((1,), (1,)), ((), ())), preferred_element_type=F32
        ).astype(BF)

    w_big[...] = jnp.zeros_like(w_big)
    for dt in range(3):
        for dy in range(3):
            taps = w_in[(3 * dt + dy) * 3 * chan : (3 * dt + dy + 1) * 3 * chan]
            for k in range(2):
                start = (4 * dt + dy + k) * slot
                w_big[start : start + 3 * chan, k * c : (k + 1) * c] = taps
    bias = jnp.concatenate([b_in[...], b_in[...]], 1)
    for p in range(rows1 // 2):
        patches = jnp.concatenate(
            [
                g[dt * width : (dt + 4) * width, 2 * p * slot : (2 * p + 4) * slot]
                for dt in range(3)
            ],
            1,
        )
        hs[p] = (dot(patches, w_big[...]) + bias).astype(BF)

    def valid(r, margin):
        at_row = tile * rows + r - margin
        return jnp.logical_and(at_row >= 0, at_row < tiles * rows)

    def normed(i, _):
        p = i // 4
        f = i % 4

        @pl.when(jnp.logical_or(f >= 2, tm > 0))
        def _():
            for k in range(2):
                r = 2 * p + k
                h0 = hs[p, pl.ds(pl.multiple_of(f * width, width), width), k * c : (k + 1) * c].astype(F32)
                gain = jnp.where(valid(r, 2), gain_one[...], 0.0)
                n1 = silu(rms(h0, gain)).astype(BF).astype(F32)
                put(v, f, r, n1)

        return 0

    lax.fori_loop(0, 2 * rows1, normed, 0)
    for f in range(2):
        for r in range(rows):
            p, k = (r + 2) // 2, (r + 2) % 2
            h0_ref[f, r] = hs[p, (f + 2) * width : (f + 3) * width, k * c : (k + 1) * c]

    @pl.when(tm == 0)
    def _():
        place = places(width, 1, True)
        for f in range(2):
            for r in range(rows1):
                if r < 2:
                    row = cache_up[f, r]
                elif r < 2 + rows:
                    row = cache_one[f, r - 2]
                else:
                    row = cache_dn[f, r - 2 - rows]
                put(v, f, r, dot(place, row))

    for j in range(4):
        pair = dot(
            jnp.concatenate([rows_of(v, 1, j, rows2), rows_of(v, 2, j, rows2)], 1),
            jnp.concatenate([both(w, u, j, 1, 0), both(w, u, j, 2, 1)], 0),
        )
        acc[j, 0] = pair[:, :c] + dot(rows_of(v, 0, j, rows2), taps_of(w, u, j, 0))
        acc[j, 1] = pair[:, c:] + dot(rows_of(v, 3, j, rows2), taps_of(w, u, j, 2))

    def finish(i, _):
        t = i // rows2
        r = i % rows2
        m = [acc[j, t, pl.ds(pl.multiple_of(r * half, half), half)] for j in range(4)]
        even = m[0] + m[1] + m[2] + b_one[...]
        odd = m[1] - m[2] - m[3] + b_one[...]
        gain = jnp.where(valid(r, 1), gain_two[...], 0.0)
        n2_ref[t, r, 0:half] = silu(rms(even, gain)).astype(BF)
        n2_ref[t, r, half:width] = silu(rms(odd, gain)).astype(BF)
        return 0

    lax.fori_loop(0, 2 * rows2, finish, 0)


def own_frames_body(n2, w, u, h0, b_two, part_ref, v, acc):
    rows2, width, c = n2.shape[1:]
    half = width // 2
    rows = rows2 - 2

    def split(i, _):
        f = i // rows2
        r = i % rows2
        put(v, f, r, n2[f, r].astype(F32))
        return 0

    lax.fori_loop(0, 2 * rows2, split, 0)
    for j in range(4):
        pair = dot(rows_of(v, 0, j, rows), both(w, u, j, 2, 1))
        acc[j, 0] = pair[:, :c]
        acc[j, 1] = pair[:, c:] + dot(rows_of(v, 1, j, rows), taps_of(w, u, j, 2))

    def finish(i, _):
        t = i // rows
        r = i % rows
        m = [acc[j, t, pl.ds(pl.multiple_of(r * half, half), half)] for j in range(4)]
        even = m[0] + m[1] + m[2] + b_two[...]
        odd = m[1] - m[2] - m[3] + b_two[...]
        part_ref[t, r, 0:half] = even + h0[t, r, 0:half].astype(F32)
        part_ref[t, r, half:width] = odd + h0[t, r, half:width].astype(F32)
        return 0

    lax.fori_loop(0, 2 * rows, finish, 0)


def earlier_frames_body(
    earlier, cache_two, cache_up, cache_dn, w, u, part, out_ref, v, acc
):
    tm = lax.axis_index("tm")
    rows2, width, c = earlier.shape[1:]
    half = width // 2
    rows = rows2 - 2

    @pl.when(tm > 0)
    def _():
        def split(i, _):
            f = i // rows2
            r = i % rows2
            put(v, f, r, earlier[f, r].astype(F32))
            return 0

        lax.fori_loop(0, 2 * rows2, split, 0)

    @pl.when(tm == 0)
    def _():
        place = places(width, 1, True)
        for f in range(2):
            for r in range(rows2):
                if r < 1:
                    row = cache_up[f, 2]
                elif r < 1 + rows:
                    row = cache_two[f, r - 1]
                else:
                    row = cache_dn[f, 2]
                put(v, f, r, dot(place, row))

    for j in range(4):
        pair = dot(rows_of(v, 1, j, rows), both(w, u, j, 1, 0))
        acc[j, 0] = pair[:, :c] + dot(rows_of(v, 0, j, rows), taps_of(w, u, j, 0))
        acc[j, 1] = pair[:, c:]

    back = places(width, 1, False)

    def finish(i, _):
        t = i // rows
        r = i % rows
        m = [acc[j, t, pl.ds(pl.multiple_of(r * half, half), half)] for j in range(4)]
        even = part[t, r, 0:half] + m[0] + m[1] + m[2]
        odd = part[t, r, half:width] + m[1] - m[2] - m[3]
        out_ref[t, r] = dot(back, jnp.concatenate([even, odd], 0).astype(BF)).astype(BF)
        return 0

    lax.fori_loop(0, 2 * rows, finish, 0)


def on_device(
    latent, cache_lat, cache_one, cache_two, w_in, b_in, gain_one, w_one, b_one, gain_two, w_two, b_two
):
    tm = lax.axis_index("tm")
    tiles = lax.axis_size("tile")
    frames, rows, width, chan = latent.shape
    c = w_in.shape[-1]
    half = width // 2

    own = jnp.swapaxes(latent, 2, 3)
    cache = jnp.swapaxes(cache_lat, 2, 3)
    prev1 = shifted(own, "tm", 1)
    prev2 = shifted(own, "tm", 2)
    prev1 = jnp.where(tm == 0, cache, prev1)
    prev2 = jnp.where(tm == 1, cache, prev2)
    six = jnp.concatenate([prev2, prev1, own], 0)
    up = shifted(six[:, rows - 3 :], "tile", 1)
    dn = shifted(six[:, :3], "tile", -1)

    caches = jnp.concatenate([cache_one[:, rows - 2 :], cache_two[:, rows - 1 :]], 1)
    cache_up = first_frames_only(caches, 1)
    caches = jnp.concatenate([cache_one[:, :2], cache_two[:, :1]], 1)
    cache_dn = first_frames_only(caches, -1)
    w1 = w_one.reshape(9, 3, c, c)
    w2 = w_two.reshape(9, 3, c, c)
    u1 = summed_kernels(w1)
    u2 = summed_kernels(w2)

    def row(x):
        return x.reshape(1, c)

    def flat(x):
        return x.reshape(-1, width)

    n2, h0 = pl.pallas_call(
        functools.partial(first_conv_body, tiles),
        out_shape=[
            jax.ShapeDtypeStruct((2, rows + 2, width, c), BF),
            jax.ShapeDtypeStruct((2, rows, width, c), BF),
        ],
        in_specs=in_vmem(15),
        out_specs=in_vmem(2),
        scratch_shapes=[
            VMEM((6, (rows + 6) * 4 * chan, width), BF),
            VMEM((6 * width, (rows + 6) * 4 * chan), BF),
            VMEM((48 * chan, 2 * c), BF),
            VMEM(((rows + 4) // 2, 4 * width, 2 * c), BF),
            VMEM((4, 4, rows + 4, half, c), BF),
            VMEM((4, 2, (rows + 2) * half, c), F32),
        ],
        compiler_params=limit(28),
        name="first_conv",
        cost_estimate=pl.CostEstimate(flops=14_000_000_000, bytes_accessed=14_000_000, transcendentals=0),
    )(
        flat(own), flat(prev1), flat(prev2), flat(up), flat(dn), cache_one, cache_up, cache_dn,
        w_in.reshape(-1, c), row(b_in), row(gain_one), w1, u1, row(b_one), row(gain_two),
    )
    earlier = shifted(n2, "tm", 1)
    part = pl.pallas_call(
        own_frames_body,
        out_shape=jax.ShapeDtypeStruct((2, rows, width, c), F32),
        in_specs=in_vmem(5),
        out_specs=in_vmem(1)[0],
        scratch_shapes=[
            VMEM((2, 4, rows + 2, half, c), BF),
            VMEM((4, 2, rows * half, c), F32),
        ],
        compiler_params=limit(16),
        name="own_frames",
        cost_estimate=pl.CostEstimate(flops=4_000_000_000, bytes_accessed=14_000_000, transcendentals=0),
    )(n2, w2, u2, h0, row(b_two))
    return pl.pallas_call(
        earlier_frames_body,
        out_shape=jax.ShapeDtypeStruct((2, rows, width, c), BF),
        in_specs=in_vmem(7),
        out_specs=in_vmem(1)[0],
        scratch_shapes=[
            VMEM((2, 4, rows + 2, half, c), BF),
            VMEM((4, 2, rows * half, c), F32),
        ],
        compiler_params=limit(16),
        name="earlier_frames",
        cost_estimate=pl.CostEstimate(flops=4_000_000_000, bytes_accessed=14_000_000, transcendentals=0),
    )(earlier, cache_two, cache_up, cache_dn, w2, u2, part)


def solution(mesh):
    return jax.shard_map(
        on_device,
        mesh=mesh,
        in_specs=(
            P("tm", "tile", None, None),
            P(None, "tile", None, None),
            P(None, "tile", None, None),
            P(None, "tile", None, None),
            P(),
            P(),
            P(),
            P(),
            P(),
            P(),
            P(),
            P(),
        ),
        out_specs=P("tm", "tile", None, None),
        check_vma=False,
    )
```

```python
import functools

import jax
import jax.numpy as jnp
from jax import lax
from jax.experimental import pallas as pl
from jax.experimental.pallas import tpu as pltpu
from jax.sharding import PartitionSpec as P

BF = jnp.bfloat16
F32 = jnp.float32
VMEM = pltpu.VMEM


def shifted(x, axis, by):
    count = lax.axis_size(axis)
    return lax.ppermute(x, axis, [(i, i + by) for i in range(count) if 0 <= i + by < count])


def first_frames_only(x, by):
    rows = lax.axis_size("tile")
    return lax.ppermute(
        x, ("tm", "tile"), [(i, i + by) for i in range(rows) if 0 <= i + by < rows]
    )


def column_of(place, width):
    half = width // 2
    return jnp.where(place < half, 2 * place, 2 * (place - half) + 1)


def silu_of_twice(h):
    return h + h * jnp.tanh(h)


def rms(v, gain):
    return v * lax.rsqrt(jnp.mean(v * v, -1, keepdims=True) + 1e-6) * gain


def filtered(even, odd):
    half = even.shape[0]
    place = lax.broadcasted_iota(jnp.int32, even.shape, 0)
    odd_before = jnp.where(place == 0, 0.0, pltpu.roll(odd, 1, 0))
    even_after = jnp.where(place == half - 1, 0.0, pltpu.roll(even, half - 1, 0))
    return (
        (odd_before - odd).astype(BF),
        (even + odd).astype(BF),
        (odd - even).astype(BF),
        (even - even_after).astype(BF),
    )


def dot(a, b):
    return jnp.dot(a, b, preferred_element_type=F32)


def in_vmem(count):
    return [pl.BlockSpec(memory_space=VMEM)] * count


def limit(mib):
    return pltpu.CompilerParams(vmem_limit_bytes=mib << 20)


def places(width, dx, transposed):
    shape = (width, width)
    to = column_of(lax.broadcasted_iota(jnp.int32, shape, 0 if transposed else 1), width)
    at = lax.broadcasted_iota(jnp.int32, shape, 1 if transposed else 0)
    return jnp.where(at == to + (dx - 1), 1.0, 0.0).astype(BF)


def put(v, f, r, row):
    half = row.shape[0] // 2
    parts = filtered(row[:half], row[half:])
    for j in range(4):
        v[f][j, r] = parts[j]


def plain_and_sums(w, u):
    return lambda j, i: w[i, 0] if j == 0 else w[i, 2] if j == 3 else u[j - 1, i]


def taps_of(w, j, dt):
    return jnp.concatenate([w(j, 3 * dt + dy) for dy in range(3)], 0)


def both(w, j, dt_a, dt_b):
    return jnp.concatenate([taps_of(w, j, dt_a), taps_of(w, j, dt_b)], 1)


def rows_of(v, f, j, at, rows):
    half, c = v[f].shape[-2:]
    return jnp.concatenate(
        [v[f][j, at + dy : at + dy + rows].reshape(rows * half, c) for dy in range(3)], 1
    )


def sum_taps(w, u, i):
    s = 0.5 * (w[i, 0].astype(F32) + w[i, 2].astype(F32))
    h = 0.5 * w[i, 1].astype(F32)
    u[0, i] = (s + h).astype(BF)
    u[1, i] = (s - h).astype(BF)


def summed_kernels_body(w, u):
    def tap(i, _):
        sum_taps(w, u, i)
        return 0

    lax.fori_loop(0, w.shape[0], tap, 0)


def summed_kernels(w):
    taps, _, c, o = w.shape
    return pl.pallas_call(
        summed_kernels_body,
        in_specs=in_vmem(1),
        out_specs=in_vmem(1)[0],
        out_shape=jax.ShapeDtypeStruct((2, taps, c, o), BF),
        compiler_params=limit(16),
        name="summed_kernels",
        cost_estimate=pl.CostEstimate(flops=6 * taps * c * o, bytes_accessed=10 * taps * c * o, transcendentals=0),
    )(w)


def border_rows_body(chan, own, prev1, prev2, cache, one, two, to_dn, to_up):
    tm = lax.axis_index("tm")
    one[...] = jnp.where(tm == 0, cache[...], prev1[...])
    two[...] = jnp.where(tm == 1, cache[...], prev2[...])
    frame = own.shape[0] // 2
    for f, src in enumerate((two, two, one, one, own, own)):
        at = (f % 2) * frame
        to_dn[f * 3 * chan : (f + 1) * 3 * chan] = src[at + frame - 3 * chan : at + frame]
        to_up[f * 3 * chan : (f + 1) * 3 * chan] = src[at : at + 3 * chan]


def border_rows(chan, own, prev1, prev2, cache):
    same = jax.ShapeDtypeStruct(own.shape, BF)
    edge = jax.ShapeDtypeStruct((18 * chan, own.shape[1]), BF)
    return pl.pallas_call(
        functools.partial(border_rows_body, chan),
        in_specs=in_vmem(4),
        out_specs=in_vmem(4),
        out_shape=[same, same, edge, edge],
        compiler_params=limit(4),
        name="border_rows",
        cost_estimate=pl.CostEstimate(flops=6_000_000_000, bytes_accessed=400_000, transcendentals=0),
    )(own, prev1, prev2, cache)


def conv_pair(v, w, acc, j, at, rows):
    c = v[0].shape[-1]
    pair = dot(
        jnp.concatenate([rows_of(v, 1, j, at, rows), rows_of(v, 2, j, at, rows)], 1),
        jnp.concatenate([both(w, j, 1, 0), both(w, j, 2, 1)], 0),
    )
    acc[j, 0] = pair[:, :c]
    acc[j, 1] = pair[:, c:]


def finish_norm(tiles, acc, b_one, gain_two, n2_ref, t, r, at):
    half = n2_ref.shape[2] // 2
    rows = pl.ds(r * half, half)
    m = [acc[j, t, rows] for j in range(4)]
    rows_here = lax.axis_index("tile")
    at_row = rows_here * (tiles[1] // tiles[0]) + at + r - 1
    keep = jnp.logical_and(at_row >= 0, at_row < tiles[1])
    gain = jnp.where(keep, 0.5 * gain_two[...], 0.0)
    even = m[0] + m[1] + m[2] + b_one[...]
    odd = m[1] - m[2] - m[3] + b_one[...]
    n2_ref[t, r, 0:half] = silu_of_twice(rms(even, gain)).astype(BF)
    n2_ref[t, r, half:] = silu_of_twice(rms(odd, gain)).astype(BF)


def conv_normed(tiles, v, w, acc, b_one, gain_two, n2_ref, at, beside):
    rows = n2_ref.shape[1]
    for n, j in enumerate((0, 3, 1, 2)):
        beside[n]()
        conv_pair(v, w, acc, j, at, rows)
    for j in range(4):
        acc[j, 0] += dot(rows_of(v, 0, j, at, rows), taps_of(w, j, 0))
    for j in range(4):
        if j < rows:
            finish_norm(tiles, acc, b_one, gain_two, n2_ref, 0, j, at)
        acc[j, 1] += dot(rows_of(v, 3, j, at, rows), taps_of(w, j, 2))
    for r in range(rows):
        finish_norm(tiles, acc, b_one, gain_two, n2_ref, 1, r, at)


def first_conv_body(
    tiles,
    own, prev1, prev2, up, dn, cache_one, cache_up, cache_dn,
    w_in, b_in, gain_one, w, u, b_one, gain_two,
    n2_ref, v0, v1, v2, v3, h0_ref,
    lats, g, w_big, hs, cached, acc,
):
    v = (v0, v1, v2, v3)
    tm = lax.axis_index("tm")
    tile = lax.axis_index("tile")
    width = own.shape[-1]
    c = w_in.shape[1]
    chan = w_in.shape[0] // 27
    rows = own.shape[0] // (2 * chan)
    rows1 = rows + 4
    slot = 4 * chan

    @pl.when(tm == 0)
    def _():
        place = places(width, 1, True)
        for f in range(2):
            for r in range(rows1):
                if r < 2:
                    row = cache_up[f, r]
                elif r < 2 + rows:
                    row = cache_one[f, r - 2]
                else:
                    row = cache_dn[f, r - 2 - rows]
                cached[f, r] = dot(place, row).astype(BF)

    lats[...] = jnp.zeros_like(lats)
    place = jnp.concatenate([places(width, dx, False) for dx in range(3)], 1)

    def lay(block, f0, r0, count):
        moved = dot(block, place).astype(BF)
        for i in range(block.shape[0] // chan):
            f, r = f0 + i // count, r0 + i % count
            for dx in range(3):
                lats[f, r * slot + dx * chan : r * slot + (dx + 1) * chan] = moved[
                    i * chan : (i + 1) * chan, dx * width : (dx + 1) * width
                ]

    lay(up[...], 0, 0, 3)
    lay(prev2[...], 0, 3, rows)
    lay(prev1[...], 2, 3, rows)
    lay(own[...], 4, 3, rows)
    lay(dn[...], 0, 3 + rows, 3)
    eye = jnp.where(
        lax.broadcasted_iota(jnp.int32, (width, width), 0)
        == lax.broadcasted_iota(jnp.int32, (width, width), 1),
        1.0,
        0.0,
    ).astype(BF)
    for f in range(6):
        g[f * width : (f + 1) * width] = lax.dot_general(
            eye, lats[f], (((1,), (1,)), ((), ())), preferred_element_type=F32
        ).astype(BF)

    w_big[...] = jnp.zeros_like(w_big)
    for dt in range(3):
        for dy in range(3):
            taps = w_in[(3 * dt + dy) * 3 * chan : (3 * dt + dy + 1) * 3 * chan]
            for k in range(2):
                start = (4 * dt + dy + k) * slot
                w_big[start : start + 3 * chan, k * c : (k + 1) * c] = taps
    bias = jnp.concatenate([b_in[...], b_in[...]], 1)

    def project(p):
        patches = jnp.concatenate(
            [
                g[dt * width : (dt + 4) * width, 2 * p * slot : (2 * p + 4) * slot]
                for dt in range(3)
            ],
            1,
        )
        hs[p] = (dot(patches, w_big[...]) + bias).astype(BF)

    def normed(f, r):
        p, k = r // 2, r % 2
        h0 = hs[p, f * width : (f + 1) * width, k * c : (k + 1) * c]
        if f >= 2 and 2 <= r < 2 + rows:
            h0_ref[f - 2, r - 2] = h0
        at_row = tile * rows + r - 2
        keep = jnp.logical_and(at_row >= 0, at_row < tiles[1])
        gain = jnp.where(keep, 0.5 * gain_one[...], 0.0)
        n1 = silu_of_twice(rms(h0.astype(F32), gain)).astype(BF).astype(F32)
        if f < 2:
            n1 = jnp.where(tm == 0, cached[f, r].astype(F32), n1)
        put(v, f, r, n1)

    part = n2_ref.shape[1]
    needed = part + 2
    pairs = rows1 // 2
    ahead = 2
    for p in range(ahead):
        project(p)
    for p in range(pairs):
        if p + ahead < pairs:
            project(p + ahead)
        for r in (2 * p, 2 * p + 1):
            if r < needed:
                for f in range(4):
                    normed(f, r)

    def rest(n):
        def work():
            for r in range(needed, rows1):
                normed(n, r)

        return work

    conv_normed(tiles, v, plain_and_sums(w, u), acc, b_one, gain_two, n2_ref, 0, [rest(n) for n in range(4)])


def second_part_body(tiles, v0, v1, v2, v3, w, u, b_one, gain_two, n2_ref, acc):
    v = (v0, v1, v2, v3)
    at = n2_ref.shape[1]
    idle = [lambda: None] * 4
    conv_normed(tiles, v, plain_and_sums(w, u), acc, b_one, gain_two, n2_ref, at, idle)


def cached_rows(cache_two, cache_up, cache_dn, first, count, cached):
    rows = cache_two.shape[1]

    @pl.when(lax.axis_index("tm") == 0)
    def _():
        place = places(cache_two.shape[2], 1, True)
        for f in range(2):
            for i in range(count):
                r = first + i
                if r < 1:
                    row = cache_up[f, 2]
                elif r < 1 + rows:
                    row = cache_two[f, r - 1]
                else:
                    row = cache_dn[f, 2]
                cached[f, i] = dot(place, row).astype(BF)


def split_earlier(v, f, earlier, cached):
    at_start = lax.axis_index("tm") == 0
    for r in range(earlier.shape[1]):
        row = jnp.where(at_start, cached[f, r].astype(F32), earlier[f, r].astype(F32))
        put(v, f, r, row)


def halves(first, second):
    return [(first, r) for r in range(first.shape[1])] + [(second, r) for r in range(second.shape[1])]


def own_frames_body(
    n2a, n2b, earlier, cache_two, cache_up, w, h0, b_two,
    part_ref, u, ve0, ve1,
    cached, v, acc,
):
    width, c = n2a.shape[2:]
    half = width // 2
    rows = part_ref.shape[1]
    source = halves(n2a, n2b)
    v = (v.at[0], v.at[1])
    cached_rows(cache_two, cache_up, None, 0, n2a.shape[1], cached)

    def split(f):
        for r, (ref, at) in enumerate(source):
            put(v, f, r, ref[f, at].astype(F32))

    def finish(t, r):
        m = [acc[j, t, r * half : (r + 1) * half] for j in range(4)]
        even = m[0] + m[1] + m[2] + b_two[...]
        odd = m[1] - m[2] - m[3] + b_two[...]
        part_ref[t, r, 0:half] = even + h0[t, r, 0:half].astype(F32)
        part_ref[t, r, half:] = odd + h0[t, r, half:].astype(F32)

    split(0)
    split(1)
    for i in range(w.shape[0]):
        sum_taps(w, u, i)
    kernel = plain_and_sums(w, u)
    for j in (0, 3, 1, 2):
        pair = dot(rows_of(v, 0, j, 0, rows), both(kernel, j, 2, 1))
        acc[j, 0] = pair[:, :c]
        acc[j, 1] = pair[:, c:]
        if j == 0:
            split_earlier((ve0, ve1), 0, earlier, cached)
        if j == 3:
            split_earlier((ve0, ve1), 1, earlier, cached)
    for j in range(4):
        if j < rows:
            finish(0, j)
        acc[j, 1] += dot(rows_of(v, 1, j, 0, rows), taps_of(kernel, j, 2))
    for r in range(rows):
        finish(1, r)


def rows_joined(first, last, f, j, rows):
    half, c = last[f].shape[-2:]
    split = first[f].shape[1]
    out = []
    for dy in range(3):
        a = first[f][j, dy:split].reshape((split - dy) * half, c)
        b = last[f][j, 0 : rows + dy - split].reshape((rows + dy - split) * half, c)
        out.append(jnp.concatenate([a, b], 0))
    return jnp.concatenate(out, 1)


def earlier_frames_body(
    ve0, ve1, earlier, cache_two, cache_dn, w, u, part, out_ref, cached, late, acc
):
    width, c = earlier.shape[2:]
    half = width // 2
    rows = out_ref.shape[1]
    kernel = plain_and_sums(w, u)
    first = (ve0, ve1)
    late = (late.at[0], late.at[1])
    cached_rows(cache_two, None, cache_dn, ve0.shape[1], earlier.shape[1], cached)
    back = places(width, 1, False)

    def finish(t, r):
        m = [acc[j, t, r * half : (r + 1) * half] for j in range(4)]
        even = part[t, r, 0:half] + m[0] + m[1] + m[2]
        odd = part[t, r, half:] + m[1] - m[2] - m[3]
        out_ref[t, r] = dot(back, jnp.concatenate([even, odd], 0).astype(BF)).astype(BF)

    split_earlier(late, 1, earlier, cached)
    for j in range(4):
        pair = dot(rows_joined(first, late, 1, j, rows), both(kernel, j, 1, 0))
        acc[j, 0] = pair[:, :c]
        acc[j, 1] = pair[:, c:]
        if j == 0:
            split_earlier(late, 0, earlier, cached)
    for j in range(4):
        if j < rows:
            finish(1, j)
        acc[j, 0] += dot(rows_joined(first, late, 0, j, rows), taps_of(kernel, j, 0))
    for r in range(rows):
        finish(0, r)


def on_device(
    latent, cache_lat, cache_one, cache_two, w_in, b_in, gain_one, w_one, b_one, gain_two, w_two, b_two
):
    frames, rows, width, chan = latent.shape
    c = w_in.shape[-1]
    half = width // 2
    part_rows = (rows + 2) // 2
    tiles = (lax.axis_size("tile"), rows * lax.axis_size("tile"))

    def flat(x):
        return x.reshape(-1, width)

    def row(x):
        return x.reshape(1, c)

    def cost(gflop):
        return pl.CostEstimate(flops=int(gflop * 1e9), bytes_accessed=int(gflop * 1e6), transcendentals=0)

    own = flat(jnp.swapaxes(latent, 2, 3))
    prev1 = shifted(own, "tm", 1)
    prev2 = shifted(own, "tm", 2)
    prev1, prev2, to_dn, to_up = border_rows(
        chan, own, prev1, prev2, flat(jnp.swapaxes(cache_lat, 2, 3))
    )
    up = shifted(to_dn, "tile", 1)
    dn = shifted(to_up, "tile", -1)
    caches = jnp.concatenate([cache_one[:, rows - 2 :], cache_two[:, rows - 1 :]], 1)
    cache_up = first_frames_only(caches, 1)
    caches = jnp.concatenate([cache_one[:, :2], cache_two[:, :1]], 1)
    cache_dn = first_frames_only(caches, -1)

    normed_part = jax.ShapeDtypeStruct((2, part_rows, width, c), BF)
    filtered_shape = (4, rows + 4, half, c)
    w1 = w_one.reshape(9, 3, c, c)
    w2 = w_two.reshape(9, 3, c, c)
    u1 = summed_kernels(w1)
    n2a, *v1, h0 = pl.pallas_call(
        functools.partial(first_conv_body, tiles),
        out_shape=[
            normed_part,
            *[jax.ShapeDtypeStruct(filtered_shape, BF)] * 4,
            jax.ShapeDtypeStruct((2, rows, width, c), BF),
        ],
        in_specs=in_vmem(15),
        out_specs=in_vmem(6),
        scratch_shapes=[
            VMEM((6, (rows + 6) * 4 * chan, width), BF),
            VMEM((6 * width, (rows + 6) * 4 * chan), BF),
            VMEM((48 * chan, 2 * c), BF),
            VMEM(((rows + 4) // 2, 4 * width, 2 * c), BF),
            VMEM((2, rows + 4, width, c), BF),
            VMEM((4, 2, part_rows * half, c), F32),
        ],
        compiler_params=limit(21),
        name="first_conv",
        cost_estimate=cost(8),
    )(
        own, prev1, prev2, up, dn, cache_one, cache_up, cache_dn,
        w_in.reshape(-1, c), row(b_in), row(gain_one), w1, u1, row(b_one), row(gain_two),
    )
    earlier_a = shifted(n2a, "tm", 1)
    n2b = pl.pallas_call(
        functools.partial(second_part_body, tiles),
        out_shape=normed_part,
        in_specs=in_vmem(8),
        out_specs=in_vmem(1)[0],
        scratch_shapes=[VMEM((4, 2, part_rows * half, c), F32)],
        compiler_params=limit(20),
        name="second_part",
        cost_estimate=cost(0.2),
    )(*v1, w1, u1, row(b_one), row(gain_two))
    earlier_b = shifted(n2b, "tm", 1)
    filtered_part = jax.ShapeDtypeStruct((4, part_rows, half, c), BF)
    part, u2, *ve = pl.pallas_call(
        own_frames_body,
        out_shape=[
            jax.ShapeDtypeStruct((2, rows, width, c), F32),
            jax.ShapeDtypeStruct((2, 9, c, c), BF),
            filtered_part,
            filtered_part,
        ],
        in_specs=in_vmem(8),
        out_specs=in_vmem(4),
        scratch_shapes=[
            VMEM((2, part_rows, width, c), BF),
            VMEM((2, 4, rows + 2, half, c), BF),
            VMEM((4, 2, rows * half, c), F32),
        ],
        compiler_params=limit(20),
        name="own_frames",
        cost_estimate=cost(4),
    )(n2a, n2b, earlier_a, cache_two, cache_up, w2, h0, row(b_two))
    return pl.pallas_call(
        earlier_frames_body,
        out_shape=jax.ShapeDtypeStruct((2, rows, width, c), BF),
        in_specs=in_vmem(8),
        out_specs=in_vmem(1)[0],
        scratch_shapes=[
            VMEM((2, part_rows, width, c), BF),
            VMEM((2, 4, part_rows, half, c), BF),
            VMEM((4, 2, rows * half, c), F32),
        ],
        compiler_params=limit(20),
        name="earlier_frames",
        cost_estimate=cost(4),
    )(*ve, earlier_b, cache_two, cache_dn, w2, u2, part)


def solution(mesh):
    return jax.shard_map(
        on_device,
        mesh=mesh,
        in_specs=(
            P("tm", "tile", None, None),
            P(None, "tile", None, None),
            P(None, "tile", None, None),
            P(None, "tile", None, None),
            P(),
            P(),
            P(),
            P(),
            P(),
            P(),
            P(),
            P(),
        ),
        out_specs=P("tm", "tile", None, None),
        check_vma=False,
    )
```

```python
import functools

import jax
import jax.numpy as jnp
from jax import lax
from jax.experimental import pallas as pl
from jax.experimental.pallas import tpu as pltpu
from jax.sharding import PartitionSpec as P

BF = jnp.bfloat16
F32 = jnp.float32
VMEM = pltpu.VMEM


def shifted(x, axis, by):
    count = lax.axis_size(axis)
    return lax.ppermute(x, axis, [(i, i + by) for i in range(count) if 0 <= i + by < count])


def first_frames_only(x, by):
    rows = lax.axis_size("tile")
    return lax.ppermute(
        x, ("tm", "tile"), [(i, i + by) for i in range(rows) if 0 <= i + by < rows]
    )


def column_of(place, width):
    half = width // 2
    return jnp.where(place < half, 2 * place, 2 * (place - half) + 1)


def silu_of_twice(h):
    return h + h * jnp.tanh(h)


def rms(v, gain):
    return v * lax.rsqrt(jnp.mean(v * v, -1, keepdims=True) + 1e-6) * gain


def filtered(even, odd):
    half, c = even.shape
    place = lax.broadcasted_iota(jnp.int32, (8, c), 0)
    odd_before = pltpu.roll(odd, 1, 0)
    odd_before = jnp.concatenate([jnp.where(place == 0, 0.0, odd_before[:8]), odd_before[8:]], 0)
    even_after = pltpu.roll(even, half - 1, 0)
    even_after = jnp.concatenate(
        [even_after[: half - 8], jnp.where(place == 7, 0.0, even_after[half - 8 :])], 0
    )
    odd_before, odd = odd_before.astype(BF), odd.astype(BF)
    even, even_after = even.astype(BF), even_after.astype(BF)
    return odd_before - odd, even + odd, odd - even, even - even_after


def dot(a, b):
    return jnp.dot(a, b, preferred_element_type=F32)


def in_vmem(count):
    return [pl.BlockSpec(memory_space=VMEM)] * count


def limit(mib):
    return pltpu.CompilerParams(vmem_limit_bytes=mib << 20)


def places(width, dx, transposed):
    shape = (width, width)
    to = column_of(lax.broadcasted_iota(jnp.int32, shape, 0 if transposed else 1), width)
    at = lax.broadcasted_iota(jnp.int32, shape, 1 if transposed else 0)
    return jnp.where(at == to + (dx - 1), 1.0, 0.0).astype(BF)


def put(v, f, r, row):
    half = row.shape[0] // 2
    parts = filtered(row[:half], row[half:])
    for j in range(4):
        v[f][j, r] = parts[j]


def plain_and_sums(w, u):
    def tap(j, i, columns):
        if j == 0 or j == 3:
            return w[i, 0 if j == 0 else 2, :, columns]
        return u[j - 1, i, :, columns]

    return tap


def taps_of(w, j, dt, columns=slice(None)):
    return jnp.concatenate([w(j, 3 * dt + dy, columns) for dy in range(3)], 0)


def weave(products, vector):
    done = 0
    for n, product in enumerate(products):
        product()
        upto = len(vector) * (n + 1) // len(products)
        for work in vector[done:upto]:
            work()
        done = upto


def pair_pieces(acc, w, j, dts, patches, add=False):
    c = acc.shape[-1]
    n = 2 * c // 3

    def piece(k):
        def product():
            lo, hi = k * n, (k + 1) * n
            kernels = []
            for dt_a, dt_b in dts:
                parts = []
                if lo < c:
                    parts.append(taps_of(w, j, dt_a, slice(lo, min(hi, c))))
                if hi > c:
                    parts.append(taps_of(w, j, dt_b, slice(max(lo, c) - c, hi - c)))
                kernels.append(jnp.concatenate(parts, 1))
            out = dot(patches(), jnp.concatenate(kernels, 0))
            if lo < c:
                acc[j, 0, :, lo : min(hi, c)] = out[:, : min(hi, c) - lo]
            if hi > c:
                here = slice(max(lo, c) - c, hi - c)
                if add:
                    acc[j, 1, :, here] += out[:, max(c - lo, 0) :]
                else:
                    acc[j, 1, :, here] = out[:, max(c - lo, 0) :]

        return product

    return [piece(k) for k in range(3)]


def single(acc, w, j, t, dt, patches, add=True):
    def product():
        out = dot(patches(), taps_of(w, j, dt))
        acc[j, t] = acc[j, t] + out if add else out

    return product


def do(function, *args):
    return lambda: function(*args)


def rows_of(v, f, j, at, rows):
    half, c = v[f].shape[-2:]
    return jnp.concatenate(
        [v[f][j, at + dy : at + dy + rows].reshape(rows * half, c) for dy in range(3)], 1
    )


def rows_joined(first, last, f, j, at, rows):
    half, c = last[f].shape[-2:]
    split = first[f].shape[1]
    out = []
    for dy in range(3):
        start, end = at + dy, at + dy + rows
        if start < split:
            a = first[f][j, start:split].reshape((split - start) * half, c)
            b = last[f][j, 0 : end - split].reshape((end - split) * half, c)
            out.append(jnp.concatenate([a, b], 0))
        else:
            out.append(last[f][j, start - split : end - split].reshape(rows * half, c))
    return jnp.concatenate(out, 1)


def sum_taps(w, u, i):
    s = 0.5 * (w[i, 0].astype(F32) + w[i, 2].astype(F32))
    h = 0.5 * w[i, 1].astype(F32)
    u[0, i] = (s + h).astype(BF)
    u[1, i] = (s - h).astype(BF)


def summed_kernels_body(w, u):
    def tap(i, _):
        sum_taps(w, u, i)
        return 0

    lax.fori_loop(0, w.shape[0], tap, 0)


def summed_kernels(w):
    taps, _, c, o = w.shape
    return pl.pallas_call(
        summed_kernels_body,
        in_specs=in_vmem(1),
        out_specs=in_vmem(1)[0],
        out_shape=jax.ShapeDtypeStruct((2, taps, c, o), BF),
        compiler_params=limit(16),
        name="summed_kernels",
        cost_estimate=pl.CostEstimate(flops=6 * taps * c * o, bytes_accessed=10 * taps * c * o, transcendentals=0),
    )(w)


def border_rows_body(chan, both, prev1, prev2, one, two, to_dn, to_up):
    size = prev1.shape[0]
    own, cache = both.at[0:size], both.at[size : 2 * size]
    tm = lax.axis_index("tm")
    one[...] = jnp.where(tm == 0, cache[...], prev1[...])
    two[...] = jnp.where(tm == 1, cache[...], prev2[...])
    frame = own.shape[0] // 2
    for f, src in enumerate((two, two, one, one, own, own)):
        at = (f % 2) * frame
        to_dn[f * 3 * chan : (f + 1) * 3 * chan] = src[at + frame - 3 * chan : at + frame]
        to_up[f * 3 * chan : (f + 1) * 3 * chan] = src[at : at + 3 * chan]


def border_rows(chan, both, prev1, prev2):
    same = jax.ShapeDtypeStruct(prev1.shape, BF)
    edge = jax.ShapeDtypeStruct((18 * chan, prev1.shape[1]), BF)
    return pl.pallas_call(
        functools.partial(border_rows_body, chan),
        in_specs=in_vmem(3),
        out_specs=in_vmem(4),
        out_shape=[same, same, edge, edge],
        compiler_params=limit(4),
        name="border_rows",
        cost_estimate=pl.CostEstimate(flops=6_000_000_000, bytes_accessed=400_000, transcendentals=0),
    )(both, prev1, prev2)


def finish_norm(tiles, acc, b_one, gain_two, n2_ref, t, r, at):
    half = n2_ref.shape[2] // 2
    rows = pl.ds(r * half, half)
    m = [acc[j, t, rows] for j in range(4)]
    rows_here = lax.axis_index("tile")
    at_row = rows_here * (tiles[1] // tiles[0]) + at + r - 1
    keep = jnp.logical_and(at_row >= 0, at_row < tiles[1])
    gain = jnp.where(keep, 0.5 * gain_two[...], 0.0)
    even = m[0] + m[1] + m[2] + b_one[...]
    odd = m[1] - m[2] - m[3] + b_one[...]
    n2_ref[t, r, 0:half] = silu_of_twice(rms(even, gain)).astype(BF)
    n2_ref[t, r, half:] = silu_of_twice(rms(odd, gain)).astype(BF)


def conv_normed(tiles, patches, w, acc, b_one, gain_two, n2_ref, at, beside_last, beside_pairs):
    rows = n2_ref.shape[1]

    def middle(j):
        return lambda: jnp.concatenate([patches(1, j), patches(2, j)], 1)

    def finish(t):
        return [
            do(finish_norm, tiles, acc, b_one, gain_two, n2_ref, t, r, at) for r in range(rows)
        ]

    weave(
        [single(acc, w, j, 1, 2, do(patches, 3, j), False) for j in range(4)],
        beside_last,
    )
    pairs = []
    for j in range(4):
        pairs += pair_pieces(acc, w, j, ((1, 0), (2, 1)), middle(j), True)
    weave(pairs, beside_pairs)
    weave([single(acc, w, j, 0, 0, do(patches, 0, j)) for j in range(4)], finish(1))
    weave([lambda: None], finish(0))


def normed_row(tiles, gain_one, hs, f, r):
    tile = lax.axis_index("tile")
    width, c = hs.shape[1] // 4, hs.shape[2] // 2
    rows = tiles[1] // tiles[0]
    p, k = r // 2, r % 2
    h0 = hs[p, f * width : (f + 1) * width, k * c : (k + 1) * c]
    at_row = tile * rows + r - 2
    keep = jnp.logical_and(at_row >= 0, at_row < tiles[1])
    gain = jnp.where(keep, 0.5 * gain_one[...], 0.0)
    return h0, silu_of_twice(rms(h0.astype(F32), gain))


def projection_body(
    tiles,
    both, prev1, prev2, up, dn, w_in, b_in, gain_one,
    hs, v2, v3, h0_ref,
    lats, g, w_big,
):
    own = both.at[0 : prev1.shape[0]]
    v = (None, None, v2, v3)
    width = own.shape[-1]
    c = w_in.shape[1]
    chan = w_in.shape[0] // 27
    rows = own.shape[0] // (2 * chan)
    rows1 = rows + 4
    slot = 4 * chan

    lats[...] = jnp.zeros_like(lats)
    place = jnp.concatenate([places(width, dx, False) for dx in range(3)], 1)

    def lay(block, f0, r0, count):
        moved = dot(block, place).astype(BF)
        for i in range(block.shape[0] // chan):
            f, r = f0 + i // count, r0 + i % count
            for dx in range(3):
                lats[f, r * slot + dx * chan : r * slot + (dx + 1) * chan] = moved[
                    i * chan : (i + 1) * chan, dx * width : (dx + 1) * width
                ]

    lay(up[...], 0, 0, 3)
    lay(prev2[...], 0, 3, rows)
    lay(prev1[...], 2, 3, rows)
    lay(own[...], 4, 3, rows)
    lay(dn[...], 0, 3 + rows, 3)
    eye = jnp.where(
        lax.broadcasted_iota(jnp.int32, (width, width), 0)
        == lax.broadcasted_iota(jnp.int32, (width, width), 1),
        1.0,
        0.0,
    ).astype(BF)
    for f in range(6):
        g[f * width : (f + 1) * width] = lax.dot_general(
            eye, lats[f], (((1,), (1,)), ((), ())), preferred_element_type=F32
        ).astype(BF)

    w_big[...] = jnp.zeros_like(w_big)
    for dt in range(3):
        for dy in range(3):
            taps = w_in[(3 * dt + dy) * 3 * chan : (3 * dt + dy + 1) * 3 * chan]
            for k in range(2):
                start = (4 * dt + dy + k) * slot
                w_big[start : start + 3 * chan, k * c : (k + 1) * c] = taps
    bias = jnp.concatenate([b_in[...], b_in[...]], 1)

    columns = 2 * c // 3

    def project(p):
        def piece(k):
            def product():
                patches = jnp.concatenate(
                    [
                        g[dt * width : (dt + 4) * width, 2 * p * slot : (2 * p + 4) * slot]
                        for dt in range(3)
                    ],
                    1,
                )
                here = slice(k * columns, (k + 1) * columns)
                hs[p, :, here] = (dot(patches, w_big[:, here]) + bias[:, here]).astype(BF)

            return product

        return [piece(k) for k in range(3)]

    def normed(f, r):
        h0, n1 = normed_row(tiles, gain_one, hs, f, r)
        if 2 <= r < 2 + rows:
            h0_ref[f - 2, r - 2] = h0
        put(v, f, r, n1)

    def units(p):
        return [do(normed, f, 2 * p + k) for k in range(2) for f in (2, 3)]

    pairs = rows1 // 2
    weave(project(0), [])
    for p in range(pairs):
        weave(project(p + 1) if p + 1 < pairs else [lambda: None], units(p))


def first_cache(cache_one, cache_up, cache_dn, first, count, cached):
    rows = cache_one.shape[1]

    @pl.when(lax.axis_index("tm") == 0)
    def _():
        place = places(cache_one.shape[2], 1, True)
        for f in range(2):
            for i in range(count):
                r = first + i
                if r < 2:
                    row = cache_up[f, r]
                elif r < 2 + rows:
                    row = cache_one[f, r - 2]
                else:
                    row = cache_dn[f, r - 2 - rows]
                cached[f, i] = dot(place, row).astype(BF)


def earlier_units(tiles, gain_one, hs, v, cached, f, first, count):
    at_start = lax.axis_index("tm") == 0

    def normed(i):
        _, n1 = normed_row(tiles, gain_one, hs, f, first + i)
        put(v, f, i, jnp.where(at_start, cached[f, i].astype(F32), n1))

    return [do(normed, i) for i in range(count)]


def first_part_body(
    tiles, hs, v2, v3, cache_one, cache_up, gain_one, w, u, b_one, gain_two,
    n2_ref, v0, v1,
    cached, acc,
):
    v = (v0, v1, v2, v3)
    rows = n2_ref.shape[1]
    needed = rows + 2
    first_cache(cache_one, cache_up, None, 0, needed, cached)

    def units(f):
        return earlier_units(tiles, gain_one, hs, v, cached, f, 0, needed)

    conv_normed(
        tiles, lambda f, j: rows_of(v, f, j, 0, rows), plain_and_sums(w, u), acc, b_one,
        gain_two, n2_ref, 0, units(1), units(0),
    )


def second_part_body(
    tiles, hs, v0, v1, v2, v3, cache_one, cache_dn, gain_one, w, u, b_one, gain_two,
    n2_ref, cached, late, acc,
):
    rows = n2_ref.shape[1]
    there = v0.shape[1]
    early, late, own = (v0, v1), (late.at[0], late.at[1]), (None, None, v2, v3)
    first_cache(cache_one, None, cache_dn, there, rows, cached)

    def patches(f, j):
        if f < 2:
            return rows_joined(early, late, f, j, rows, rows)
        return rows_of(own, f, j, rows, rows)

    def units(f):
        return earlier_units(tiles, gain_one, hs, late, cached, f, there, rows)

    conv_normed(
        tiles, patches, plain_and_sums(w, u), acc, b_one, gain_two, n2_ref, rows,
        units(1), units(0),
    )


def cached_rows(cache_two, cache_up, cache_dn, first, count, cached):
    rows = cache_two.shape[1]

    @pl.when(lax.axis_index("tm") == 0)
    def _():
        place = places(cache_two.shape[2], 1, True)
        for f in range(2):
            for i in range(count):
                r = first + i
                if r < 1:
                    row = cache_up[f, 2]
                elif r < 1 + rows:
                    row = cache_two[f, r - 1]
                else:
                    row = cache_dn[f, 2]
                cached[f, i] = dot(place, row).astype(BF)


def split_earlier(v, f, earlier, cached):
    at_start = lax.axis_index("tm") == 0

    def split(r):
        row = jnp.where(at_start, cached[f, r].astype(F32), earlier[f, r].astype(F32))
        put(v, f, r, row)

    return [do(split, r) for r in range(earlier.shape[1])]


def halves(first, second):
    return [(first, r) for r in range(first.shape[1])] + [(second, r) for r in range(second.shape[1])]


def own_frames_body(
    n2a, n2b, earlier, cache_two, cache_up, w, u, h0, b_two,
    part_ref, ve0, ve1,
    cached, v, acc,
):
    width, c = n2a.shape[2:]
    half = width // 2
    rows = part_ref.shape[1]
    source = halves(n2a, n2b)
    v = (v.at[0], v.at[1])
    cached_rows(cache_two, cache_up, None, 0, n2a.shape[1], cached)

    def split(f):
        return [
            do(lambda r, ref, at: put(v, f, r, ref[f, at].astype(F32)), r, ref, at)
            for r, (ref, at) in enumerate(source)
        ]

    def finish(t, r):
        m = [acc[j, t, r * half : (r + 1) * half] for j in range(4)]
        even = m[0] + m[1] + m[2] + b_two[...]
        odd = m[1] - m[2] - m[3] + b_two[...]
        part_ref[t, r, 0:half] = even + h0[t, r, 0:half].astype(F32)
        part_ref[t, r, half:] = odd + h0[t, r, half:].astype(F32)

    kernel = plain_and_sums(w, u)

    def pair(j):
        return pair_pieces(acc, kernel, j, ((2, 1),), do(rows_of, v, 0, j, 0, rows))

    def other(j):
        return single(acc, kernel, j, 1, 2, do(rows_of, v, 1, j, 0, rows))

    ve = (ve0, ve1)
    weave([lambda: None], split(0))
    weave(pair(0) + pair(1), split(1))
    weave(
        pair(2) + pair(3),
        split_earlier(ve, 0, earlier, cached) + split_earlier(ve, 1, earlier, cached),
    )
    weave([other(j) for j in range(4)], [do(finish, 0, r) for r in range(rows)])
    weave([lambda: None], [do(finish, 1, r) for r in range(rows)])


def earlier_frames_body(
    ve0, ve1, earlier, cache_two, cache_dn, w, u, part, out_ref, cached, late, acc
):
    width, c = earlier.shape[2:]
    half = width // 2
    rows = out_ref.shape[1]
    kernel = plain_and_sums(w, u)
    first = (ve0, ve1)
    late = (late.at[0], late.at[1])
    cached_rows(cache_two, None, cache_dn, ve0.shape[1], earlier.shape[1], cached)
    back = places(width, 1, False)

    def finish(t, r):
        m = [acc[j, t, r * half : (r + 1) * half] for j in range(4)]
        even = part[t, r, 0:half] + m[0] + m[1] + m[2]
        odd = part[t, r, half:] + m[1] - m[2] - m[3]
        out_ref[t, r] = dot(back, jnp.concatenate([even, odd], 0).astype(BF)).astype(BF)

    weave([lambda: None], split_earlier(late, 1, earlier, cached))
    pairs = []
    for j in range(4):
        pairs += pair_pieces(acc, kernel, j, ((1, 0),), do(rows_joined, first, late, 1, j, 0, rows))
    weave(pairs, split_earlier(late, 0, earlier, cached))
    weave(
        [single(acc, kernel, j, 0, 0, do(rows_joined, first, late, 0, j, 0, rows)) for j in range(4)],
        [do(finish, 1, r) for r in range(rows)],
    )
    weave([lambda: None], [do(finish, 0, r) for r in range(rows)])


def on_device(
    latent, cache_lat, cache_one, cache_two, w_in, b_in, gain_one, w_one, b_one, gain_two, w_two, b_two
):
    frames, rows, width, chan = latent.shape
    c = w_in.shape[-1]
    half = width // 2
    part_rows = (rows + 2) // 2
    tiles = (lax.axis_size("tile"), rows * lax.axis_size("tile"))

    def flat(x):
        return x.reshape(-1, width)

    def row(x):
        return x.reshape(1, c)

    def cost(gflop):
        return pl.CostEstimate(flops=int(gflop * 1e9), bytes_accessed=int(gflop * 1e6), transcendentals=0)

    own = flat(jnp.swapaxes(latent, 2, 3))
    prev1 = shifted(own, "tm", 1)
    prev2 = shifted(own, "tm", 2)
    own_and_cache = jnp.concatenate([own, flat(jnp.swapaxes(cache_lat, 2, 3))], 0)
    prev1, prev2, to_dn, to_up = border_rows(chan, own_and_cache, prev1, prev2)
    up = shifted(to_dn, "tile", 1)
    dn = shifted(to_up, "tile", -1)
    caches = jnp.concatenate([cache_one[:, rows - 2 :], cache_two[:, rows - 1 :]], 1)
    cache_up = first_frames_only(caches, 1)
    caches = jnp.concatenate([cache_one[:, :2], cache_two[:, :1]], 1)
    cache_dn = first_frames_only(caches, -1)

    normed_part = jax.ShapeDtypeStruct((2, part_rows, width, c), BF)
    w1 = w_one.reshape(9, 3, c, c)
    w2 = w_two.reshape(9, 3, c, c)
    u1 = summed_kernels(w1)
    u2 = summed_kernels(w2)
    filtered = jax.ShapeDtypeStruct((4, rows + 4, half, c), BF)
    hs, *v_own, h0 = pl.pallas_call(
        functools.partial(projection_body, tiles),
        out_shape=[
            jax.ShapeDtypeStruct(((rows + 4) // 2, 4 * width, 2 * c), BF),
            filtered,
            filtered,
            jax.ShapeDtypeStruct((2, rows, width, c), BF),
        ],
        in_specs=in_vmem(8),
        out_specs=in_vmem(4),
        scratch_shapes=[
            VMEM((6, (rows + 6) * 4 * chan, width), BF),
            VMEM((6 * width, (rows + 6) * 4 * chan), BF),
            VMEM((48 * chan, 2 * c), BF),
        ],
        compiler_params=limit(16),
        name="projection",
        cost_estimate=cost(6),
    )(own_and_cache, prev1, prev2, up, dn, w_in.reshape(-1, c), row(b_in), row(gain_one))
    n2a, *v_earlier = pl.pallas_call(
        functools.partial(first_part_body, tiles),
        out_shape=[normed_part, *[jax.ShapeDtypeStruct((4, part_rows + 2, half, c), BF)] * 2],
        in_specs=in_vmem(10),
        out_specs=in_vmem(3),
        scratch_shapes=[
            VMEM((2, part_rows + 2, width, c), BF),
            VMEM((4, 2, part_rows * half, c), F32),
        ],
        compiler_params=limit(20),
        name="first_part",
        cost_estimate=cost(8),
    )(
        hs, *v_own, cache_one, cache_up, row(gain_one),
        w1, u1, row(b_one), row(gain_two),
    )
    earlier_a = shifted(n2a, "tm", 1)
    n2b = pl.pallas_call(
        functools.partial(second_part_body, tiles),
        out_shape=normed_part,
        in_specs=in_vmem(12),
        out_specs=in_vmem(1)[0],
        scratch_shapes=[
            VMEM((2, part_rows, width, c), BF),
            VMEM((2, 4, part_rows, half, c), BF),
            VMEM((4, 2, part_rows * half, c), F32),
        ],
        compiler_params=limit(20),
        name="second_part",
        cost_estimate=cost(0.2),
    )(
        hs, *v_earlier, *v_own, cache_one, cache_dn, row(gain_one),
        w1, u1, row(b_one), row(gain_two),
    )
    earlier_b = shifted(n2b, "tm", 1)
    filtered_part = jax.ShapeDtypeStruct((4, part_rows, half, c), BF)
    part, *ve = pl.pallas_call(
        own_frames_body,
        out_shape=[
            jax.ShapeDtypeStruct((2, rows, width, c), F32),
            filtered_part,
            filtered_part,
        ],
        in_specs=in_vmem(9),
        out_specs=in_vmem(3),
        scratch_shapes=[
            VMEM((2, part_rows, width, c), BF),
            VMEM((2, 4, rows + 2, half, c), BF),
            VMEM((4, 2, rows * half, c), F32),
        ],
        compiler_params=limit(20),
        name="own_frames",
        cost_estimate=cost(4),
    )(n2a, n2b, earlier_a, cache_two, cache_up, w2, u2, h0, row(b_two))
    return pl.pallas_call(
        earlier_frames_body,
        out_shape=jax.ShapeDtypeStruct((2, rows, width, c), BF),
        in_specs=in_vmem(8),
        out_specs=in_vmem(1)[0],
        scratch_shapes=[
            VMEM((2, part_rows, width, c), BF),
            VMEM((2, 4, part_rows, half, c), BF),
            VMEM((4, 2, rows * half, c), F32),
        ],
        compiler_params=limit(20),
        name="earlier_frames",
        cost_estimate=cost(4),
    )(*ve, earlier_b, cache_two, cache_dn, w2, u2, part)


def solution(mesh):
    return jax.shard_map(
        on_device,
        mesh=mesh,
        in_specs=(
            P("tm", "tile", None, None),
            P(None, "tile", None, None),
            P(None, "tile", None, None),
            P(None, "tile", None, None),
            P(),
            P(),
            P(),
            P(),
            P(),
            P(),
            P(),
            P(),
        ),
        out_specs=P("tm", "tile", None, None),
        check_vma=False,
    )
```

```python
import functools

import jax
import jax.numpy as jnp
from jax import lax
from jax.experimental import pallas as pl
from jax.experimental.pallas import tpu as pltpu
from jax.sharding import PartitionSpec as P

BF = jnp.bfloat16
F32 = jnp.float32
VMEM = pltpu.VMEM


def shifted(x, axis, by):
    count = lax.axis_size(axis)
    return lax.ppermute(x, axis, [(i, i + by) for i in range(count) if 0 <= i + by < count])


def first_frames_only(x, by):
    rows = lax.axis_size("tile")
    return lax.ppermute(
        x, ("tm", "tile"), [(i, i + by) for i in range(rows) if 0 <= i + by < rows]
    )


def column_of(place, width):
    half = width // 2
    return jnp.where(place < half, 2 * place, 2 * (place - half) + 1)


def silu_of_twice(h):
    return h + h * jnp.tanh(h)


def rms(v, gain):
    return v * lax.rsqrt(jnp.mean(v * v, -1, keepdims=True) + 1e-6) * gain


def filtered(even, odd):
    half, c = even.shape
    place = lax.broadcasted_iota(jnp.int32, (8, c), 0)
    odd_before = pltpu.roll(odd, 1, 0)
    odd_before = jnp.concatenate([jnp.where(place == 0, 0.0, odd_before[:8]), odd_before[8:]], 0)
    even_after = pltpu.roll(even, half - 1, 0)
    even_after = jnp.concatenate(
        [even_after[: half - 8], jnp.where(place == 7, 0.0, even_after[half - 8 :])], 0
    )
    odd_before, odd = odd_before.astype(BF), odd.astype(BF)
    even, even_after = even.astype(BF), even_after.astype(BF)
    return odd_before - odd, even + odd, odd - even, even - even_after


def dot(a, b):
    return jnp.dot(a, b, preferred_element_type=F32)


def in_vmem(count):
    return [pl.BlockSpec(memory_space=VMEM)] * count


def limit(mib):
    return pltpu.CompilerParams(vmem_limit_bytes=mib << 20)


def places(width, dx, transposed):
    shape = (width, width)
    to = column_of(lax.broadcasted_iota(jnp.int32, shape, 0 if transposed else 1), width)
    at = lax.broadcasted_iota(jnp.int32, shape, 1 if transposed else 0)
    return jnp.where(at == to + (dx - 1), 1.0, 0.0).astype(BF)


def put(v, f, r, row):
    half = row.shape[0] // 2
    parts = filtered(row[:half], row[half:])
    for j in range(4):
        v[f][j, r] = parts[j]


def plain_and_sums(w, u):
    def tap(j, i, columns):
        if j == 0 or j == 3:
            return w[i, 0 if j == 0 else 2, :, columns]
        return u[j - 1, i, :, columns]

    return tap


def taps_of(w, j, dt, columns=slice(None)):
    return jnp.concatenate([w(j, 3 * dt + dy, columns) for dy in range(3)], 0)


def weave(products, vector):
    done = 0
    for n, product in enumerate(products):
        product()
        upto = len(vector) * (n + 1) // len(products)
        for work in vector[done:upto]:
            work()
        done = upto


def pair_pieces(acc, w, j, dts, patches, add=False):
    c = acc.shape[-1]
    n = 2 * c // 3

    def piece(k):
        def product():
            lo, hi = k * n, (k + 1) * n
            kernels = []
            for dt_a, dt_b in dts:
                parts = []
                if lo < c:
                    parts.append(taps_of(w, j, dt_a, slice(lo, min(hi, c))))
                if hi > c:
                    parts.append(taps_of(w, j, dt_b, slice(max(lo, c) - c, hi - c)))
                kernels.append(jnp.concatenate(parts, 1))
            out = dot(patches(), jnp.concatenate(kernels, 0))
            if lo < c:
                acc[j, 0, :, lo : min(hi, c)] = out[:, : min(hi, c) - lo]
            if hi > c:
                here = slice(max(lo, c) - c, hi - c)
                if add:
                    acc[j, 1, :, here] += out[:, max(c - lo, 0) :]
                else:
                    acc[j, 1, :, here] = out[:, max(c - lo, 0) :]

        return product

    return [piece(k) for k in range(3)]


def single(acc, w, j, t, dt, patches, add=True):
    def product():
        out = dot(patches(), taps_of(w, j, dt))
        acc[j, t] = acc[j, t] + out if add else out

    return product


def do(function, *args):
    return lambda: function(*args)


def rows_of(v, f, j, at, rows):
    half, c = v[f].shape[-2:]
    return jnp.concatenate(
        [v[f][j, at + dy : at + dy + rows].reshape(rows * half, c) for dy in range(3)], 1
    )


def rows_joined(first, last, f, j, at, rows):
    half, c = last[f].shape[-2:]
    split = first[f].shape[1]
    out = []
    for dy in range(3):
        start, end = at + dy, at + dy + rows
        if start < split:
            a = first[f][j, start:split].reshape((split - start) * half, c)
            b = last[f][j, 0 : end - split].reshape((end - split) * half, c)
            out.append(jnp.concatenate([a, b], 0))
        else:
            out.append(last[f][j, start - split : end - split].reshape(rows * half, c))
    return jnp.concatenate(out, 1)


def sum_taps(w, u, i):
    s = 0.5 * (w[i, 0].astype(F32) + w[i, 2].astype(F32))
    h = 0.5 * w[i, 1].astype(F32)
    u[0, i] = (s + h).astype(BF)
    u[1, i] = (s - h).astype(BF)


def summed_kernels_body(w, u):
    def tap(i, _):
        sum_taps(w, u, i)
        return 0

    lax.fori_loop(0, w.shape[0], tap, 0)


def first_kernels_body(w, w_in, cache_one, cache_two, u, w_big, placed_one, placed_two):
    summed_kernels_body(w, u)

    @pl.when(lax.axis_index("tm") == 0)
    def _():
        place = places(cache_one.shape[2], 1, True)
        for source, placed in ((cache_one, placed_one), (cache_two, placed_two)):
            for f in range(source.shape[0]):
                for r in range(source.shape[1]):
                    placed[f, r] = dot(place, source[f, r]).astype(BF)

    c = w_in.shape[1]
    chan = w_in.shape[0] // 27
    slot = 4 * chan
    w_big[...] = jnp.zeros_like(w_big)
    for dt in range(3):
        for dy in range(3):
            taps = w_in[(3 * dt + dy) * 3 * chan : (3 * dt + dy + 1) * 3 * chan]
            for k in range(2):
                start = (4 * dt + dy + k) * slot
                w_big[start : start + 3 * chan, k * c : (k + 1) * c] = taps


def first_kernels(w, w_in, cache_one, cache_two):
    taps, _, c, o = w.shape
    chan = w_in.shape[0] // 27
    return pl.pallas_call(
        first_kernels_body,
        in_specs=in_vmem(4),
        out_specs=in_vmem(4),
        out_shape=[
            jax.ShapeDtypeStruct((2, taps, c, o), BF),
            jax.ShapeDtypeStruct((48 * chan, 2 * c), BF),
            jax.ShapeDtypeStruct(cache_one.shape, BF),
            jax.ShapeDtypeStruct(cache_two.shape, BF),
        ],
        compiler_params=limit(16),
        name="first_kernels",
        cost_estimate=pl.CostEstimate(flops=6 * taps * c * o, bytes_accessed=10 * taps * c * o, transcendentals=0),
    )(w, w_in, cache_one, cache_two)


def summed_kernels(w):
    taps, _, c, o = w.shape
    return pl.pallas_call(
        summed_kernels_body,
        in_specs=in_vmem(1),
        out_specs=in_vmem(1)[0],
        out_shape=jax.ShapeDtypeStruct((2, taps, c, o), BF),
        compiler_params=limit(16),
        name="summed_kernels",
        cost_estimate=pl.CostEstimate(flops=6 * taps * c * o, bytes_accessed=10 * taps * c * o, transcendentals=0),
    )(w)


def border_rows_body(chan, both, prev1, prev2, one, two, to_dn, to_up):
    size = prev1.shape[0]
    own, cache = both.at[0:size], both.at[size : 2 * size]
    tm = lax.axis_index("tm")
    one[...] = jnp.where(tm == 0, cache[...], prev1[...])
    two[...] = jnp.where(tm == 1, cache[...], prev2[...])
    frame = own.shape[0] // 2
    for f, src in enumerate((two, two, one, one, own, own)):
        at = (f % 2) * frame
        to_dn[f * 3 * chan : (f + 1) * 3 * chan] = src[at + frame - 3 * chan : at + frame]
        to_up[f * 3 * chan : (f + 1) * 3 * chan] = src[at : at + 3 * chan]


def border_rows(chan, both, prev1, prev2):
    same = jax.ShapeDtypeStruct(prev1.shape, BF)
    edge = jax.ShapeDtypeStruct((18 * chan, prev1.shape[1]), BF)
    return pl.pallas_call(
        functools.partial(border_rows_body, chan),
        in_specs=in_vmem(3),
        out_specs=in_vmem(4),
        out_shape=[same, same, edge, edge],
        compiler_params=limit(4),
        name="border_rows",
        cost_estimate=pl.CostEstimate(flops=6_000_000_000, bytes_accessed=400_000, transcendentals=0),
    )(both, prev1, prev2)


def finish_norm(tiles, acc, b_one, gain_two, n2_ref, t, r, at):
    half = n2_ref.shape[2] // 2
    rows = pl.ds(r * half, half)
    m = [acc[j, t, rows] for j in range(4)]
    rows_here = lax.axis_index("tile")
    at_row = rows_here * (tiles[1] // tiles[0]) + at + r - 1
    keep = jnp.logical_and(at_row >= 0, at_row < tiles[1])
    gain = jnp.where(keep, 0.5 * gain_two[...], 0.0)
    even = m[0] + m[1] + m[2] + b_one[...]
    odd = m[1] - m[2] - m[3] + b_one[...]
    n2_ref[t, r, 0:half] = silu_of_twice(rms(even, gain)).astype(BF)
    n2_ref[t, r, half:] = silu_of_twice(rms(odd, gain)).astype(BF)


def conv_normed(tiles, patches, w, acc, b_one, gain_two, n2_ref, at, beside_last, beside_pairs):
    rows = n2_ref.shape[1]

    def middle(j):
        return lambda: jnp.concatenate([patches(1, j), patches(2, j)], 1)

    def finish(t):
        return [
            do(finish_norm, tiles, acc, b_one, gain_two, n2_ref, t, r, at) for r in range(rows)
        ]

    weave(
        [single(acc, w, j, 1, 2, do(patches, 3, j), False) for j in range(4)],
        beside_last,
    )
    pairs = []
    for j in range(4):
        pairs += pair_pieces(acc, w, j, ((1, 0), (2, 1)), middle(j), True)
    weave(pairs, beside_pairs)
    weave([single(acc, w, j, 0, 0, do(patches, 0, j)) for j in range(4)], finish(1))
    weave([lambda: None], finish(0))


def normed_row(tiles, gain_one, hs, f, r):
    tile = lax.axis_index("tile")
    width, c = hs.shape[1] // 4, hs.shape[2] // 2
    rows = tiles[1] // tiles[0]
    p, k = r // 2, r % 2
    h0 = hs[p, f * width : (f + 1) * width, k * c : (k + 1) * c]
    at_row = tile * rows + r - 2
    keep = jnp.logical_and(at_row >= 0, at_row < tiles[1])
    gain = jnp.where(keep, 0.5 * gain_one[...], 0.0)
    return h0, silu_of_twice(rms(h0.astype(F32), gain))


def projection_body(
    tiles,
    both, prev1, prev2, up, dn, w_big, b_in, gain_one,
    hs, v2, v3, h0_ref,
    lats, g,
):
    own = both.at[0 : prev1.shape[0]]
    v = (None, None, v2, v3)
    width = own.shape[-1]
    c = w_big.shape[1] // 2
    chan = w_big.shape[0] // 48
    rows = own.shape[0] // (2 * chan)
    rows1 = rows + 4
    slot = 4 * chan

    empty = jnp.zeros((6, chan, width), BF)
    for r in range(rows + 6):
        lats[:, (r + 1) * slot - chan : (r + 1) * slot] = empty
    place = jnp.concatenate([places(width, dx, False) for dx in range(3)], 1)

    def lay(block, f0, r0, count):
        moved = dot(block, place).astype(BF)
        for i in range(block.shape[0] // chan):
            f, r = f0 + i // count, r0 + i % count
            for dx in range(3):
                lats[f, r * slot + dx * chan : r * slot + (dx + 1) * chan] = moved[
                    i * chan : (i + 1) * chan, dx * width : (dx + 1) * width
                ]

    lay(up[...], 0, 0, 3)
    lay(prev2[...], 0, 3, rows)
    lay(prev1[...], 2, 3, rows)
    lay(own[...], 4, 3, rows)
    lay(dn[...], 0, 3 + rows, 3)
    eye = jnp.where(
        lax.broadcasted_iota(jnp.int32, (width, width), 0)
        == lax.broadcasted_iota(jnp.int32, (width, width), 1),
        1.0,
        0.0,
    ).astype(BF)
    for f in range(6):
        g[f * width : (f + 1) * width] = lax.dot_general(
            eye, lats[f], (((1,), (1,)), ((), ())), preferred_element_type=F32
        ).astype(BF)

    bias = jnp.concatenate([b_in[...], b_in[...]], 1)

    columns = 2 * c // 3

    def project(p):
        def piece(k):
            def product():
                patches = jnp.concatenate(
                    [
                        g[dt * width : (dt + 4) * width, 2 * p * slot : (2 * p + 4) * slot]
                        for dt in range(3)
                    ],
                    1,
                )
                here = slice(k * columns, (k + 1) * columns)
                hs[p, :, here] = (dot(patches, w_big[:, here]) + bias[:, here]).astype(BF)

            return product

        return [piece(k) for k in range(3)]

    def normed(f, r):
        h0, n1 = normed_row(tiles, gain_one, hs, f, r)
        if 2 <= r < 2 + rows:
            h0_ref[f - 2, r - 2] = h0
        put(v, f, r, n1)

    def units(p):
        return [do(normed, f, 2 * p + k) for k in range(2) for f in (2, 3)]

    pairs = rows1 // 2
    weave(project(0), [])
    for p in range(pairs):
        weave(project(p + 1) if p + 1 < pairs else [lambda: None], units(p))


def place_border(border, first, count, cached):
    @pl.when(lax.axis_index("tm") == 0)
    def _():
        place = places(border.shape[2], 1, True)
        for f in range(2):
            for i in range(count):
                cached[f, i] = dot(place, border[f, first + i]).astype(BF)


def earlier_units(tiles, gain_one, hs, v, source, f, first, count):
    at_start = lax.axis_index("tm") == 0

    def normed(i):
        _, n1 = normed_row(tiles, gain_one, hs, f, first + i)
        put(v, f, i, jnp.where(at_start, source(f, first + i).astype(F32), n1))

    return [do(normed, i) for i in range(count)]


def first_part_body(
    tiles, hs, v2, v3, placed, cache_up, gain_one, w, u, b_one, gain_two,
    n2_ref, v0, v1,
    cached, acc,
):
    v = (v0, v1, v2, v3)
    rows = n2_ref.shape[1]
    needed = rows + 2
    place_border(cache_up, 0, 2, cached)

    def source(f, r):
        return cached[f, r] if r < 2 else placed[f, r - 2]

    def units(f):
        return earlier_units(tiles, gain_one, hs, v, source, f, 0, needed)

    conv_normed(
        tiles, lambda f, j: rows_of(v, f, j, 0, rows), plain_and_sums(w, u), acc, b_one,
        gain_two, n2_ref, 0, units(1), units(0),
    )


def second_part_body(
    tiles, hs, v0, v1, v2, v3, placed, cache_dn, gain_one, w, u, b_one, gain_two,
    n2_ref, cached, late, acc,
):
    rows = n2_ref.shape[1]
    there = v0.shape[1]
    early, late, own = (v0, v1), (late.at[0], late.at[1]), (None, None, v2, v3)
    here = placed.shape[1] + 2
    place_border(cache_dn, 0, 2, cached)

    def source(f, r):
        return placed[f, r - 2] if r < here else cached[f, r - here]

    def patches(f, j):
        if f < 2:
            return rows_joined(early, late, f, j, rows, rows)
        return rows_of(own, f, j, rows, rows)

    def units(f):
        return earlier_units(tiles, gain_one, hs, late, source, f, there, rows)

    conv_normed(
        tiles, patches, plain_and_sums(w, u), acc, b_one, gain_two, n2_ref, rows,
        units(1), units(0),
    )


def split_earlier(v, f, earlier, source, first):
    at_start = lax.axis_index("tm") == 0

    def split(r):
        row = jnp.where(at_start, source(f, first + r).astype(F32), earlier[f, r].astype(F32))
        put(v, f, r, row)

    return [do(split, r) for r in range(earlier.shape[1])]


def halves(first, second):
    return [(first, r) for r in range(first.shape[1])] + [(second, r) for r in range(second.shape[1])]


def own_frames_body(
    n2a, n2b, earlier, placed, cache_up, w, u, h0, b_two,
    part_ref, ve0, ve1,
    cached, v, acc,
):
    width, c = n2a.shape[2:]
    half = width // 2
    rows = part_ref.shape[1]
    source = halves(n2a, n2b)
    v = (v.at[0], v.at[1])
    place_border(cache_up, 2, 1, cached)

    def cache_row(f, r):
        return cached[f, 0] if r < 1 else placed[f, r - 1]

    def split(f):
        return [
            do(lambda r, ref, at: put(v, f, r, ref[f, at].astype(F32)), r, ref, at)
            for r, (ref, at) in enumerate(source)
        ]

    def finish(t, r):
        m = [acc[j, t, r * half : (r + 1) * half] for j in range(4)]
        even = m[0] + m[1] + m[2] + b_two[...]
        odd = m[1] - m[2] - m[3] + b_two[...]
        part_ref[t, r, 0:half] = even + h0[t, r, 0:half].astype(F32)
        part_ref[t, r, half:] = odd + h0[t, r, half:].astype(F32)

    kernel = plain_and_sums(w, u)

    def pair(j):
        return pair_pieces(acc, kernel, j, ((2, 1),), do(rows_of, v, 0, j, 0, rows))

    def other(j):
        return single(acc, kernel, j, 1, 2, do(rows_of, v, 1, j, 0, rows))

    ve = (ve0, ve1)
    weave([lambda: None], split(0))
    weave(pair(0) + pair(1), split(1))
    weave(
        pair(2) + pair(3),
        split_earlier(ve, 0, earlier, cache_row, 0) + split_earlier(ve, 1, earlier, cache_row, 0),
    )
    weave([other(j) for j in range(4)], [do(finish, 0, r) for r in range(rows)])
    weave([lambda: None], [do(finish, 1, r) for r in range(rows)])


def earlier_frames_body(
    ve0, ve1, earlier, placed, cache_dn, w, u, part, out_ref, cached, late, acc
):
    width, c = earlier.shape[2:]
    half = width // 2
    rows = out_ref.shape[1]
    kernel = plain_and_sums(w, u)
    first = (ve0, ve1)
    late = (late.at[0], late.at[1])
    place_border(cache_dn, 2, 1, cached)
    there = ve0.shape[1]

    def cache_row(f, r):
        return placed[f, r - 1] if r < 1 + rows else cached[f, 0]

    back = places(width, 1, False)

    def finish(t, r):
        m = [acc[j, t, r * half : (r + 1) * half] for j in range(4)]
        even = part[t, r, 0:half] + m[0] + m[1] + m[2]
        odd = part[t, r, half:] + m[1] - m[2] - m[3]
        out_ref[t, r] = dot(back, jnp.concatenate([even, odd], 0).astype(BF)).astype(BF)

    weave([lambda: None], split_earlier(late, 1, earlier, cache_row, there))
    pairs = []
    for j in range(4):
        pairs += pair_pieces(acc, kernel, j, ((1, 0),), do(rows_joined, first, late, 1, j, 0, rows))
    weave(pairs, split_earlier(late, 0, earlier, cache_row, there))
    weave(
        [single(acc, kernel, j, 0, 0, do(rows_joined, first, late, 0, j, 0, rows)) for j in range(4)],
        [do(finish, 1, r) for r in range(rows)],
    )
    weave([lambda: None], [do(finish, 0, r) for r in range(rows)])


def on_device(
    latent, cache_lat, cache_one, cache_two, w_in, b_in, gain_one, w_one, b_one, gain_two, w_two, b_two
):
    frames, rows, width, chan = latent.shape
    c = w_in.shape[-1]
    half = width // 2
    part_rows = (rows + 2) // 2
    tiles = (lax.axis_size("tile"), rows * lax.axis_size("tile"))

    def flat(x):
        return x.reshape(-1, width)

    def row(x):
        return x.reshape(1, c)

    def cost(gflop):
        return pl.CostEstimate(flops=int(gflop * 1e9), bytes_accessed=int(gflop * 1e6), transcendentals=0)

    own = flat(jnp.swapaxes(latent, 2, 3))
    prev1 = shifted(own, "tm", 1)
    prev2 = shifted(own, "tm", 2)
    own_and_cache = jnp.concatenate([own, flat(jnp.swapaxes(cache_lat, 2, 3))], 0)
    prev1, prev2, to_dn, to_up = border_rows(chan, own_and_cache, prev1, prev2)
    up = shifted(to_dn, "tile", 1)
    dn = shifted(to_up, "tile", -1)
    caches = jnp.concatenate([cache_one[:, rows - 2 :], cache_two[:, rows - 1 :]], 1)
    cache_up = first_frames_only(caches, 1)
    caches = jnp.concatenate([cache_one[:, :2], cache_two[:, :1]], 1)
    cache_dn = first_frames_only(caches, -1)

    normed_part = jax.ShapeDtypeStruct((2, part_rows, width, c), BF)
    w1 = w_one.reshape(9, 3, c, c)
    w2 = w_two.reshape(9, 3, c, c)
    u1, w_big, placed_one, placed_two = first_kernels(
        w1, w_in.reshape(-1, c), cache_one, cache_two
    )
    u2 = summed_kernels(w2)
    filtered = jax.ShapeDtypeStruct((4, rows + 4, half, c), BF)
    hs, *v_own, h0 = pl.pallas_call(
        functools.partial(projection_body, tiles),
        out_shape=[
            jax.ShapeDtypeStruct(((rows + 4) // 2, 4 * width, 2 * c), BF),
            filtered,
            filtered,
            jax.ShapeDtypeStruct((2, rows, width, c), BF),
        ],
        in_specs=in_vmem(8),
        out_specs=in_vmem(4),
        scratch_shapes=[
            VMEM((6, (rows + 6) * 4 * chan, width), BF),
            VMEM((6 * width, (rows + 6) * 4 * chan), BF),
        ],
        compiler_params=limit(16),
        name="projection",
        cost_estimate=cost(6),
    )(own_and_cache, prev1, prev2, up, dn, w_big, row(b_in), row(gain_one))
    n2a, *v_earlier = pl.pallas_call(
        functools.partial(first_part_body, tiles),
        out_shape=[normed_part, *[jax.ShapeDtypeStruct((4, part_rows + 2, half, c), BF)] * 2],
        in_specs=in_vmem(10),
        out_specs=in_vmem(3),
        scratch_shapes=[
            VMEM((2, 2, width, c), BF),
            VMEM((4, 2, part_rows * half, c), F32),
        ],
        compiler_params=limit(20),
        name="first_part",
        cost_estimate=cost(8),
    )(
        hs, *v_own, placed_one, cache_up, row(gain_one),
        w1, u1, row(b_one), row(gain_two),
    )
    earlier_a = shifted(n2a, "tm", 1)
    n2b = pl.pallas_call(
        functools.partial(second_part_body, tiles),
        out_shape=normed_part,
        in_specs=in_vmem(12),
        out_specs=in_vmem(1)[0],
        scratch_shapes=[
            VMEM((2, 2, width, c), BF),
            VMEM((2, 4, part_rows, half, c), BF),
            VMEM((4, 2, part_rows * half, c), F32),
        ],
        compiler_params=limit(20),
        name="second_part",
        cost_estimate=cost(0.2),
    )(
        hs, *v_earlier, *v_own, placed_one, cache_dn, row(gain_one),
        w1, u1, row(b_one), row(gain_two),
    )
    earlier_b = shifted(n2b, "tm", 1)
    filtered_part = jax.ShapeDtypeStruct((4, part_rows, half, c), BF)
    part, *ve = pl.pallas_call(
        own_frames_body,
        out_shape=[
            jax.ShapeDtypeStruct((2, rows, width, c), F32),
            filtered_part,
            filtered_part,
        ],
        in_specs=in_vmem(9),
        out_specs=in_vmem(3),
        scratch_shapes=[
            VMEM((2, 2, width, c), BF),
            VMEM((2, 4, rows + 2, half, c), BF),
            VMEM((4, 2, rows * half, c), F32),
        ],
        compiler_params=limit(20),
        name="own_frames",
        cost_estimate=cost(4),
    )(n2a, n2b, earlier_a, placed_two, cache_up, w2, u2, h0, row(b_two))
    return pl.pallas_call(
        earlier_frames_body,
        out_shape=jax.ShapeDtypeStruct((2, rows, width, c), BF),
        in_specs=in_vmem(8),
        out_specs=in_vmem(1)[0],
        scratch_shapes=[
            VMEM((2, 2, width, c), BF),
            VMEM((2, 4, part_rows, half, c), BF),
            VMEM((4, 2, rows * half, c), F32),
        ],
        compiler_params=limit(20),
        name="earlier_frames",
        cost_estimate=cost(4),
    )(*ve, earlier_b, placed_two, cache_dn, w2, u2, part)


def solution(mesh):
    return jax.shard_map(
        on_device,
        mesh=mesh,
        in_specs=(
            P("tm", "tile", None, None),
            P(None, "tile", None, None),
            P(None, "tile", None, None),
            P(None, "tile", None, None),
            P(),
            P(),
            P(),
            P(),
            P(),
            P(),
            P(),
            P(),
        ),
        out_specs=P("tm", "tile", None, None),
        check_vma=False,
    )
```

```python
import functools

import jax
import jax.numpy as jnp
from jax import lax
from jax.experimental import pallas as pl
from jax.experimental.pallas import tpu as pltpu
from jax.sharding import PartitionSpec as P

BF = jnp.bfloat16
F32 = jnp.float32
VMEM = pltpu.VMEM


def shifted(x, axis, by):
    count = lax.axis_size(axis)
    return lax.ppermute(x, axis, [(i, i + by) for i in range(count) if 0 <= i + by < count])


def first_frames_only(x, by):
    rows = lax.axis_size("tile")
    return lax.ppermute(
        x, ("tm", "tile"), [(i, i + by) for i in range(rows) if 0 <= i + by < rows]
    )


def column_of(place, width):
    half = width // 2
    return jnp.where(place < half, 2 * place, 2 * (place - half) + 1)


def silu_of_twice(h):
    return h + h * jnp.tanh(h)


def rms(v, gain):
    return v * lax.rsqrt(jnp.mean(v * v, -1, keepdims=True) + 1e-6) * gain


def filtered(even, odd):
    half, c = even.shape
    place = lax.broadcasted_iota(jnp.int32, (8, c), 0)
    odd_before = pltpu.roll(odd, 1, 0)
    odd_before = jnp.concatenate([jnp.where(place == 0, 0.0, odd_before[:8]), odd_before[8:]], 0)
    even_after = pltpu.roll(even, half - 1, 0)
    even_after = jnp.concatenate(
        [even_after[: half - 8], jnp.where(place == 7, 0.0, even_after[half - 8 :])], 0
    )
    odd_before, odd = odd_before.astype(BF), odd.astype(BF)
    even, even_after = even.astype(BF), even_after.astype(BF)
    return odd_before - odd, even + odd, odd - even, even - even_after


def dot(a, b):
    return jnp.dot(a, b, preferred_element_type=F32)


def in_vmem(count):
    return [pl.BlockSpec(memory_space=VMEM)] * count


def limit(mib):
    return pltpu.CompilerParams(vmem_limit_bytes=mib << 20)


def places(width, dx, transposed):
    shape = (width, width)
    to = column_of(lax.broadcasted_iota(jnp.int32, shape, 0 if transposed else 1), width)
    at = lax.broadcasted_iota(jnp.int32, shape, 1 if transposed else 0)
    return jnp.where(at == to + (dx - 1), 1.0, 0.0).astype(BF)


def put(v, f, r, row):
    half = row.shape[0] // 2
    parts = filtered(row[:half], row[half:])
    for j in range(4):
        v[f][j, r] = parts[j]


def plain_and_sums(w, u):
    def tap(j, i, columns):
        if j == 0 or j == 3:
            return w[i, 0 if j == 0 else 2, :, columns]
        return u[j - 1, i, :, columns]

    return tap


def taps_of(w, j, dt, columns=slice(None)):
    return jnp.concatenate([w(j, 3 * dt + dy, columns) for dy in range(3)], 0)


def weave(products, vector):
    done = 0
    for n, product in enumerate(products):
        product()
        upto = len(vector) * (n + 1) // len(products)
        for work in vector[done:upto]:
            work()
        done = upto


def pair_pieces(acc, w, j, dts, patches, add=False):
    c = acc.shape[-1]
    n = 2 * c // 3

    def piece(k):
        def product():
            lo, hi = k * n, (k + 1) * n
            kernels = []
            for dt_a, dt_b in dts:
                parts = []
                if lo < c:
                    parts.append(taps_of(w, j, dt_a, slice(lo, min(hi, c))))
                if hi > c:
                    parts.append(taps_of(w, j, dt_b, slice(max(lo, c) - c, hi - c)))
                kernels.append(jnp.concatenate(parts, 1))
            out = dot(patches(), jnp.concatenate(kernels, 0))
            if lo < c:
                acc[j, 0, :, lo : min(hi, c)] = out[:, : min(hi, c) - lo]
            if hi > c:
                here = slice(max(lo, c) - c, hi - c)
                if add:
                    acc[j, 1, :, here] += out[:, max(c - lo, 0) :]
                else:
                    acc[j, 1, :, here] = out[:, max(c - lo, 0) :]

        return product

    return [piece(k) for k in range(3)]


def single(acc, w, j, t, dt, patches, add=True):
    def product():
        out = dot(patches(), taps_of(w, j, dt))
        acc[j, t] = acc[j, t] + out if add else out

    return product


def do(function, *args):
    return lambda: function(*args)


def rows_of(v, f, j, at, rows):
    half, c = v[f].shape[-2:]
    return jnp.concatenate(
        [v[f][j, at + dy : at + dy + rows].reshape(rows * half, c) for dy in range(3)], 1
    )


def rows_joined(first, last, f, j, at, rows):
    half, c = last[f].shape[-2:]
    split = first[f].shape[1]
    out = []
    for dy in range(3):
        start, end = at + dy, at + dy + rows
        if end <= split:
            out.append(first[f][j, start:end].reshape(rows * half, c))
        elif start < split:
            a = first[f][j, start:split].reshape((split - start) * half, c)
            b = last[f][j, 0 : end - split].reshape((end - split) * half, c)
            out.append(jnp.concatenate([a, b], 0))
        else:
            out.append(last[f][j, start - split : end - split].reshape(rows * half, c))
    return jnp.concatenate(out, 1)


def sum_taps(w, u, i):
    s = 0.5 * (w[i, 0].astype(F32) + w[i, 2].astype(F32))
    h = 0.5 * w[i, 1].astype(F32)
    u[0, i] = (s + h).astype(BF)
    u[1, i] = (s - h).astype(BF)


def summed_kernels_body(w, u):
    def tap(i, _):
        sum_taps(w, u, i)
        return 0

    lax.fori_loop(0, w.shape[0], tap, 0)


def first_kernels_body(w, w_in, cache_one, cache_two, u, w_big, placed_one, placed_two):
    summed_kernels_body(w, u)

    @pl.when(lax.axis_index("tm") == 0)
    def _():
        place = places(cache_one.shape[2], 1, True)
        for source, placed in ((cache_one, placed_one), (cache_two, placed_two)):
            for f in range(source.shape[0]):
                for r in range(source.shape[1]):
                    placed[f, r] = dot(place, source[f, r]).astype(BF)

    c = w_in.shape[1]
    chan = w_in.shape[0] // 27
    slot = 4 * chan
    w_big[...] = jnp.zeros_like(w_big)
    for dt in range(3):
        for dy in range(3):
            taps = w_in[(3 * dt + dy) * 3 * chan : (3 * dt + dy + 1) * 3 * chan]
            for k in range(2):
                start = (4 * dt + dy + k) * slot
                w_big[start : start + 3 * chan, k * c : (k + 1) * c] = taps


def first_kernels(w, w_in, cache_one, cache_two):
    taps, _, c, o = w.shape
    chan = w_in.shape[0] // 27
    return pl.pallas_call(
        first_kernels_body,
        in_specs=in_vmem(4),
        out_specs=in_vmem(4),
        out_shape=[
            jax.ShapeDtypeStruct((2, taps, c, o), BF),
            jax.ShapeDtypeStruct((48 * chan, 2 * c), BF),
            jax.ShapeDtypeStruct(cache_one.shape, BF),
            jax.ShapeDtypeStruct(cache_two.shape, BF),
        ],
        compiler_params=limit(16),
        name="first_kernels",
        cost_estimate=pl.CostEstimate(flops=6 * taps * c * o, bytes_accessed=10 * taps * c * o, transcendentals=0),
    )(w, w_in, cache_one, cache_two)


def summed_kernels(w):
    taps, _, c, o = w.shape
    return pl.pallas_call(
        summed_kernels_body,
        in_specs=in_vmem(1),
        out_specs=in_vmem(1)[0],
        out_shape=jax.ShapeDtypeStruct((2, taps, c, o), BF),
        compiler_params=limit(16),
        name="summed_kernels",
        cost_estimate=pl.CostEstimate(flops=6 * taps * c * o, bytes_accessed=10 * taps * c * o, transcendentals=0),
    )(w)


def border_rows_body(chan, both, prev1, prev2, one, two, to_dn, to_up):
    size = prev1.shape[0]
    own, cache = both.at[0:size], both.at[size : 2 * size]
    tm = lax.axis_index("tm")
    one[...] = jnp.where(tm == 0, cache[...], prev1[...])
    two[...] = jnp.where(tm == 1, cache[...], prev2[...])
    frame = own.shape[0] // 2
    for f, src in enumerate((two, two, one, one, own, own)):
        at = (f % 2) * frame
        to_dn[f * 3 * chan : (f + 1) * 3 * chan] = src[at + frame - 3 * chan : at + frame]
        to_up[f * 3 * chan : (f + 1) * 3 * chan] = src[at : at + 3 * chan]


def border_rows(chan, both, prev1, prev2):
    same = jax.ShapeDtypeStruct(prev1.shape, BF)
    edge = jax.ShapeDtypeStruct((18 * chan, prev1.shape[1]), BF)
    return pl.pallas_call(
        functools.partial(border_rows_body, chan),
        in_specs=in_vmem(3),
        out_specs=in_vmem(4),
        out_shape=[same, same, edge, edge],
        compiler_params=limit(4),
        name="border_rows",
        cost_estimate=pl.CostEstimate(flops=6_000_000_000, bytes_accessed=400_000, transcendentals=0),
    )(both, prev1, prev2)


def finish_norm(tiles, acc, b_one, gain_two, n2_ref, t, r, at):
    half = n2_ref.shape[2] // 2
    rows = pl.ds(r * half, half)
    m = [acc[j, t, rows] for j in range(4)]
    rows_here = lax.axis_index("tile")
    at_row = rows_here * (tiles[1] // tiles[0]) + at + r - 1
    keep = jnp.logical_and(at_row >= 0, at_row < tiles[1])
    gain = jnp.where(keep, 0.5 * gain_two[...], 0.0)
    even = m[0] + m[1] + m[2] + b_one[...]
    odd = m[1] - m[2] - m[3] + b_one[...]
    n2_ref[t, r, 0:half] = silu_of_twice(rms(even, gain)).astype(BF)
    n2_ref[t, r, half:] = silu_of_twice(rms(odd, gain)).astype(BF)


def conv_normed(tiles, patches, w, acc, b_one, gain_two, n2_ref, at, beside_last, beside_pairs):
    rows = n2_ref.shape[1]

    def middle(j):
        return lambda: jnp.concatenate([patches(1, j), patches(2, j)], 1)

    def finish(t):
        return [
            do(finish_norm, tiles, acc, b_one, gain_two, n2_ref, t, r, at) for r in range(rows)
        ]

    weave(
        [single(acc, w, j, 1, 2, do(patches, 3, j), False) for j in range(4)],
        beside_last,
    )
    pairs = []
    for j in range(4):
        pairs += pair_pieces(acc, w, j, ((1, 0), (2, 1)), middle(j), True)
    weave(pairs, beside_pairs)
    weave([single(acc, w, j, 0, 0, do(patches, 0, j)) for j in range(4)], finish(1))
    weave([lambda: None], finish(0))


def normed_row(tiles, gain_one, hs, f, r):
    tile = lax.axis_index("tile")
    width, c = hs.shape[1] // 4, hs.shape[2] // 2
    rows = tiles[1] // tiles[0]
    p, k = r // 2, r % 2
    h0 = hs[p, f * width : (f + 1) * width, k * c : (k + 1) * c]
    at_row = tile * rows + r - 2
    keep = jnp.logical_and(at_row >= 0, at_row < tiles[1])
    gain = jnp.where(keep, 0.5 * gain_one[...], 0.0)
    return h0, silu_of_twice(rms(h0.astype(F32), gain))


def projection_body(
    tiles,
    both, prev1, prev2, up, dn, w_big, b_in, gain_one,
    hs, v2, v3, h0_ref,
    lats, g,
):
    own = both.at[0 : prev1.shape[0]]
    v = (None, None, v2, v3)
    width = own.shape[-1]
    c = w_big.shape[1] // 2
    chan = w_big.shape[0] // 48
    rows = own.shape[0] // (2 * chan)
    rows1 = rows + 4
    slot = 4 * chan

    empty = jnp.zeros((6, chan, width), BF)
    for r in range(rows + 6):
        lats[:, (r + 1) * slot - chan : (r + 1) * slot] = empty
    place = jnp.concatenate([places(width, dx, False) for dx in range(3)], 1)

    def lay(block, f0, r0, count):
        moved = dot(block, place).astype(BF)
        for i in range(block.shape[0] // chan):
            f, r = f0 + i // count, r0 + i % count
            for dx in range(3):
                lats[f, r * slot + dx * chan : r * slot + (dx + 1) * chan] = moved[
                    i * chan : (i + 1) * chan, dx * width : (dx + 1) * width
                ]

    lay(up[...], 0, 0, 3)
    lay(prev2[...], 0, 3, rows)
    lay(prev1[...], 2, 3, rows)
    lay(own[...], 4, 3, rows)
    lay(dn[...], 0, 3 + rows, 3)
    eye = jnp.where(
        lax.broadcasted_iota(jnp.int32, (width, width), 0)
        == lax.broadcasted_iota(jnp.int32, (width, width), 1),
        1.0,
        0.0,
    ).astype(BF)
    for f in range(6):
        g[f * width : (f + 1) * width] = lax.dot_general(
            eye, lats[f], (((1,), (1,)), ((), ())), preferred_element_type=F32
        ).astype(BF)

    bias = jnp.concatenate([b_in[...], b_in[...]], 1)

    columns = 2 * c // 3

    def project(p):
        def piece(k):
            def product():
                patches = jnp.concatenate(
                    [
                        g[dt * width : (dt + 4) * width, 2 * p * slot : (2 * p + 4) * slot]
                        for dt in range(3)
                    ],
                    1,
                )
                here = slice(k * columns, (k + 1) * columns)
                hs[p, :, here] = (dot(patches, w_big[:, here]) + bias[:, here]).astype(BF)

            return product

        return [piece(k) for k in range(3)]

    def normed(f, r):
        h0, n1 = normed_row(tiles, gain_one, hs, f, r)
        if 2 <= r < 2 + rows:
            h0_ref[f - 2, r - 2] = h0
        put(v, f, r, n1)

    def units(p):
        return [do(normed, f, 2 * p + k) for k in range(2) for f in (2, 3)]

    pairs = rows1 // 2
    weave(project(0), [])
    for p in range(pairs):
        weave(project(p + 1) if p + 1 < pairs else [lambda: None], units(p))


def place_border(border, first, count, cached):
    @pl.when(lax.axis_index("tm") == 0)
    def _():
        place = places(border.shape[2], 1, True)
        for f in range(2):
            for i in range(count):
                cached[f, i] = dot(place, border[f, first + i]).astype(BF)


def earlier_units(tiles, gain_one, hs, v, source, f, first, count):
    at_start = lax.axis_index("tm") == 0

    def normed(i):
        _, n1 = normed_row(tiles, gain_one, hs, f, first + i)
        put(v, f, i, jnp.where(at_start, source(f, first + i).astype(F32), n1))

    return [do(normed, i) for i in range(count)]


def first_part_body(
    tiles, hs, v2, v3, placed, cache_up, gain_one, w, u, b_one, gain_two,
    n2_ref, v0, v1,
    cached, acc,
):
    v = (v0, v1, v2, v3)
    rows = n2_ref.shape[1]
    needed = rows + 2
    place_border(cache_up, 0, 2, cached)

    def source(f, r):
        return cached[f, r] if r < 2 else placed[f, r - 2]

    def units(f):
        return earlier_units(tiles, gain_one, hs, v, source, f, 0, needed)

    conv_normed(
        tiles, lambda f, j: rows_of(v, f, j, 0, rows), plain_and_sums(w, u), acc, b_one,
        gain_two, n2_ref, 0, units(1), units(0),
    )


def second_part_body(
    tiles, hs, v0, v1, v2, v3, placed, cache_dn, gain_one, w, u, b_one, gain_two,
    n2_ref, cached, late, acc,
):
    rows = n2_ref.shape[1]
    there = v0.shape[1]
    early, late, own = (v0, v1), (late.at[0], late.at[1]), (None, None, v2, v3)
    here = placed.shape[1] + 2
    place_border(cache_dn, 0, 2, cached)

    def source(f, r):
        return placed[f, r - 2] if r < here else cached[f, r - here]

    def patches(f, j):
        if f < 2:
            return rows_joined(early, late, f, j, rows, rows)
        return rows_of(own, f, j, rows, rows)

    def units(f):
        return earlier_units(tiles, gain_one, hs, late, source, f, there, rows)

    conv_normed(
        tiles, patches, plain_and_sums(w, u), acc, b_one, gain_two, n2_ref, rows,
        units(1), units(0),
    )


def split_earlier(v, f, earlier, source, first):
    at_start = lax.axis_index("tm") == 0

    def split(r):
        row = jnp.where(at_start, source(f, first + r).astype(F32), earlier[f, r].astype(F32))
        put(v, f, r, row)

    return [do(split, r) for r in range(earlier.shape[1])]


def halves(first, second):
    return [(first, r) for r in range(first.shape[1])] + [(second, r) for r in range(second.shape[1])]


def own_frames_body(
    n2a, n2b, earlier, placed, cache_up, w, u, h0, b_two,
    part_ref, ve0, ve1,
    cached, v, acc,
):
    width, c = n2a.shape[2:]
    half = width // 2
    rows = part_ref.shape[1]
    source = halves(n2a, n2b)
    v = (v.at[0], v.at[1])
    place_border(cache_up, 2, 1, cached)

    def cache_row(f, r):
        return cached[f, 0] if r < 1 else placed[f, r - 1]

    def split(f):
        return [
            do(lambda r, ref, at: put(v, f, r, ref[f, at].astype(F32)), r, ref, at)
            for r, (ref, at) in enumerate(source)
        ]

    def finish(t, r):
        m = [acc[j, t, r * half : (r + 1) * half] for j in range(4)]
        even = m[0] + m[1] + m[2] + b_two[...]
        odd = m[1] - m[2] - m[3] + b_two[...]
        part_ref[t, r, 0:half] = even + h0[t, r, 0:half].astype(F32)
        part_ref[t, r, half:] = odd + h0[t, r, half:].astype(F32)

    kernel = plain_and_sums(w, u)

    def pair(j):
        return pair_pieces(acc, kernel, j, ((2, 1),), do(rows_of, v, 0, j, 0, rows))

    def other(j):
        return single(acc, kernel, j, 1, 2, do(rows_of, v, 1, j, 0, rows))

    ve = (ve0, ve1)
    weave([lambda: None], split(0))
    weave(pair(0) + pair(1), split(1))
    weave(
        pair(2) + pair(3),
        split_earlier(ve, 0, earlier, cache_row, 0) + split_earlier(ve, 1, earlier, cache_row, 0),
    )
    weave([other(j) for j in range(4)], [do(finish, 0, r) for r in range(rows)])
    weave([lambda: None], [do(finish, 1, r) for r in range(rows)])


def earlier_frames_body(
    ve0, ve1, earlier, placed, cache_dn, w, u, part, out_ref, cached, late, acc, columns
):
    width, c = earlier.shape[2:]
    half = width // 2
    rows = out_ref.shape[1]
    kernel = plain_and_sums(w, u)
    first = (ve0, ve1)
    late = (late.at[0], late.at[1])
    place_border(cache_dn, 2, 1, cached)
    there = ve0.shape[1]

    def cache_row(f, r):
        return placed[f, r - 1] if r < 1 + rows else cached[f, 0]


    def finish(t, r):
        m = [acc[j, t, r * half : (r + 1) * half] for j in range(4)]
        even = part[t, r, 0:half] + m[0] + m[1] + m[2]
        odd = part[t, r, half:] + m[1] - m[2] - m[3]
        for k in range(c // 128):
            lanes = slice(k * 128, (k + 1) * 128)
            row = columns.at[(t * rows + r) * (c // 128) + k]
            row[pl.ds(0, half, stride=2)] = even[:, lanes]
            row[pl.ds(1, half, stride=2)] = odd[:, lanes]
            out_ref[t, r, :, lanes] = row[...].astype(BF)

    weave([lambda: None], split_earlier(late, 1, earlier, cache_row, there))
    pairs = []
    for j in range(4):
        pairs += pair_pieces(acc, kernel, j, ((1, 0),), do(rows_joined, first, late, 1, j, 0, rows))
    weave(pairs, split_earlier(late, 0, earlier, cache_row, there))
    weave(
        [single(acc, kernel, j, 0, 0, do(rows_joined, first, late, 0, j, 0, rows)) for j in range(4)],
        [do(finish, 1, r) for r in range(rows)],
    )
    weave([lambda: None], [do(finish, 0, r) for r in range(rows)])


def on_device(
    latent, cache_lat, cache_one, cache_two, w_in, b_in, gain_one, w_one, b_one, gain_two, w_two, b_two
):
    frames, rows, width, chan = latent.shape
    c = w_in.shape[-1]
    half = width // 2
    part_rows = (rows + 2) // 2
    tiles = (lax.axis_size("tile"), rows * lax.axis_size("tile"))

    def flat(x):
        return x.reshape(-1, width)

    def row(x):
        return x.reshape(1, c)

    def cost(gflop):
        return pl.CostEstimate(flops=int(gflop * 1e9), bytes_accessed=int(gflop * 1e6), transcendentals=0)

    own = flat(jnp.swapaxes(latent, 2, 3))
    prev1 = shifted(own, "tm", 1)
    prev2 = shifted(own, "tm", 2)
    own_and_cache = jnp.concatenate([own, flat(jnp.swapaxes(cache_lat, 2, 3))], 0)
    prev1, prev2, to_dn, to_up = border_rows(chan, own_and_cache, prev1, prev2)
    up = shifted(to_dn, "tile", 1)
    dn = shifted(to_up, "tile", -1)
    caches = jnp.concatenate([cache_one[:, rows - 2 :], cache_two[:, rows - 1 :]], 1)
    cache_up = first_frames_only(caches, 1)
    caches = jnp.concatenate([cache_one[:, :2], cache_two[:, :1]], 1)
    cache_dn = first_frames_only(caches, -1)

    normed_part = jax.ShapeDtypeStruct((2, part_rows, width, c), BF)
    w1 = w_one.reshape(9, 3, c, c)
    w2 = w_two.reshape(9, 3, c, c)
    u1, w_big, placed_one, placed_two = first_kernels(
        w1, w_in.reshape(-1, c), cache_one, cache_two
    )
    u2 = summed_kernels(w2)
    filtered = jax.ShapeDtypeStruct((4, rows + 4, half, c), BF)
    hs, *v_own, h0 = pl.pallas_call(
        functools.partial(projection_body, tiles),
        out_shape=[
            jax.ShapeDtypeStruct(((rows + 4) // 2, 4 * width, 2 * c), BF),
            filtered,
            filtered,
            jax.ShapeDtypeStruct((2, rows, width, c), BF),
        ],
        in_specs=in_vmem(8),
        out_specs=in_vmem(4),
        scratch_shapes=[
            VMEM((6, (rows + 6) * 4 * chan, width), BF),
            VMEM((6 * width, (rows + 6) * 4 * chan), BF),
        ],
        compiler_params=limit(16),
        name="projection",
        cost_estimate=cost(6),
    )(own_and_cache, prev1, prev2, up, dn, w_big, row(b_in), row(gain_one))
    n2a, *v_earlier = pl.pallas_call(
        functools.partial(first_part_body, tiles),
        out_shape=[normed_part, *[jax.ShapeDtypeStruct((4, part_rows + 2, half, c), BF)] * 2],
        in_specs=in_vmem(10),
        out_specs=in_vmem(3),
        scratch_shapes=[
            VMEM((2, 2, width, c), BF),
            VMEM((4, 2, part_rows * half, c), F32),
        ],
        compiler_params=limit(20),
        name="first_part",
        cost_estimate=cost(8),
    )(
        hs, *v_own, placed_one, cache_up, row(gain_one),
        w1, u1, row(b_one), row(gain_two),
    )
    earlier_a = shifted(n2a, "tm", 1)
    n2b = pl.pallas_call(
        functools.partial(second_part_body, tiles),
        out_shape=normed_part,
        in_specs=in_vmem(12),
        out_specs=in_vmem(1)[0],
        scratch_shapes=[
            VMEM((2, 2, width, c), BF),
            VMEM((2, 4, part_rows, half, c), BF),
            VMEM((4, 2, part_rows * half, c), F32),
        ],
        compiler_params=limit(20),
        name="second_part",
        cost_estimate=cost(0.2),
    )(
        hs, *v_earlier, *v_own, placed_one, cache_dn, row(gain_one),
        w1, u1, row(b_one), row(gain_two),
    )
    earlier_b = shifted(n2b, "tm", 1)
    filtered_part = jax.ShapeDtypeStruct((4, part_rows, half, c), BF)
    part, *ve = pl.pallas_call(
        own_frames_body,
        out_shape=[
            jax.ShapeDtypeStruct((2, rows, width, c), F32),
            filtered_part,
            filtered_part,
        ],
        in_specs=in_vmem(9),
        out_specs=in_vmem(3),
        scratch_shapes=[
            VMEM((2, 2, width, c), BF),
            VMEM((2, 4, rows + 2, half, c), BF),
            VMEM((4, 2, rows * half, c), F32),
        ],
        compiler_params=limit(20),
        name="own_frames",
        cost_estimate=cost(4),
    )(n2a, n2b, earlier_a, placed_two, cache_up, w2, u2, h0, row(b_two))
    return pl.pallas_call(
        earlier_frames_body,
        out_shape=jax.ShapeDtypeStruct((2, rows, width, c), BF),
        in_specs=in_vmem(8),
        out_specs=in_vmem(1)[0],
        scratch_shapes=[
            VMEM((2, 2, width, c), BF),
            VMEM((2, 4, part_rows, half, c), BF),
            VMEM((4, 2, rows * half, c), F32),
            VMEM((2 * rows * (c // 128), width, 128), F32),
        ],
        compiler_params=limit(20),
        name="earlier_frames",
        cost_estimate=cost(4),
    )(*ve, earlier_b, placed_two, cache_dn, w2, u2, part)


def solution(mesh):
    return jax.shard_map(
        on_device,
        mesh=mesh,
        in_specs=(
            P("tm", "tile", None, None),
            P(None, "tile", None, None),
            P(None, "tile", None, None),
            P(None, "tile", None, None),
            P(),
            P(),
            P(),
            P(),
            P(),
            P(),
            P(),
            P(),
        ),
        out_specs=P("tm", "tile", None, None),
        check_vma=False,
    )
```

```python
import functools

import jax
import jax.numpy as jnp
from jax import lax
from jax.experimental import pallas as pl
from jax.experimental.pallas import tpu as pltpu
from jax.sharding import PartitionSpec as P

BF = jnp.bfloat16
F32 = jnp.float32
VMEM = pltpu.VMEM


def shifted(x, axis, by):
    count = lax.axis_size(axis)
    return lax.ppermute(x, axis, [(i, i + by) for i in range(count) if 0 <= i + by < count])


def first_frames_only(x, by):
    rows = lax.axis_size("tile")
    return lax.ppermute(
        x, ("tm", "tile"), [(i, i + by) for i in range(rows) if 0 <= i + by < rows]
    )


def column_of(place, width):
    half = width // 2
    return jnp.where(place < half, 2 * place, 2 * (place - half) + 1)


def silu_of_twice(h):
    return h + h * jnp.tanh(h)


def rms(v, gain):
    return v * lax.rsqrt(jnp.mean(v * v, -1, keepdims=True) + 1e-6) * gain


def filtered(even, odd):
    half, c = even.shape
    place = lax.broadcasted_iota(jnp.int32, (8, c), 0)
    odd_before = pltpu.roll(odd, 1, 0)
    odd_before = jnp.concatenate([jnp.where(place == 0, 0.0, odd_before[:8]), odd_before[8:]], 0)
    even_after = pltpu.roll(even, half - 1, 0)
    even_after = jnp.concatenate(
        [even_after[: half - 8], jnp.where(place == 7, 0.0, even_after[half - 8 :])], 0
    )
    odd_before, odd = odd_before.astype(BF), odd.astype(BF)
    even, even_after = even.astype(BF), even_after.astype(BF)
    return odd_before - odd, 0.5 * (even + odd), 0.5 * (odd - even), even - even_after


def dot(a, b):
    return jnp.dot(a, b, preferred_element_type=F32)


def in_vmem(count):
    return [pl.BlockSpec(memory_space=VMEM)] * count


def limit(mib):
    return pltpu.CompilerParams(vmem_limit_bytes=mib << 20)


def places(width, dx, transposed):
    shape = (width, width)
    to = column_of(lax.broadcasted_iota(jnp.int32, shape, 0 if transposed else 1), width)
    at = lax.broadcasted_iota(jnp.int32, shape, 1 if transposed else 0)
    return jnp.where(at == to + (dx - 1), 1.0, 0.0).astype(BF)


def put(v, f, r, row):
    half = row.shape[0] // 2
    parts = filtered(row[:half], row[half:])
    for j in range(4):
        v[f][j, r] = parts[j]


def plain_and_sums(w, u):
    def tap(j, i, columns):
        if j == 0 or j == 3:
            return w[i, 0 if j == 0 else 2, :, columns]
        return u[j - 1, i, :, columns]

    return tap


def taps_of(w, j, dt, columns=slice(None)):
    return jnp.concatenate([w(j, 3 * dt + dy, columns) for dy in range(3)], 0)


def weave(products, vector):
    done = 0
    for n, product in enumerate(products):
        product()
        upto = len(vector) * (n + 1) // len(products)
        for work in vector[done:upto]:
            work()
        done = upto


def pair_pieces(acc, w, j, dts, patches, add=False):
    c = acc.shape[-1]
    n = 2 * c // 3

    def piece(k):
        def product():
            lo, hi = k * n, (k + 1) * n
            kernels = []
            for dt_a, dt_b in dts:
                parts = []
                if lo < c:
                    parts.append(taps_of(w, j, dt_a, slice(lo, min(hi, c))))
                if hi > c:
                    parts.append(taps_of(w, j, dt_b, slice(max(lo, c) - c, hi - c)))
                kernels.append(jnp.concatenate(parts, 1))
            out = dot(patches(), jnp.concatenate(kernels, 0))
            if lo < c:
                acc[j, 0, :, lo : min(hi, c)] = out[:, : min(hi, c) - lo]
            if hi > c:
                here = slice(max(lo, c) - c, hi - c)
                if add:
                    acc[j, 1, :, here] += out[:, max(c - lo, 0) :]
                else:
                    acc[j, 1, :, here] = out[:, max(c - lo, 0) :]

        return product

    return [piece(k) for k in range(3)]


def single(acc, w, j, t, dt, patches, add=True):
    def product():
        out = dot(patches(), taps_of(w, j, dt))
        acc[j, t] = acc[j, t] + out if add else out

    return product


def do(function, *args):
    return lambda: function(*args)


def rows_of(v, f, j, at, rows):
    half, c = v[f].shape[-2:]
    return jnp.concatenate(
        [v[f][j, at + dy : at + dy + rows].reshape(rows * half, c) for dy in range(3)], 1
    )


def rows_joined(first, last, f, j, at, rows):
    half, c = last[f].shape[-2:]
    split = first[f].shape[1]
    out = []
    for dy in range(3):
        start, end = at + dy, at + dy + rows
        if end <= split:
            out.append(first[f][j, start:end].reshape(rows * half, c))
        elif start < split:
            a = first[f][j, start:split].reshape((split - start) * half, c)
            b = last[f][j, 0 : end - split].reshape((end - split) * half, c)
            out.append(jnp.concatenate([a, b], 0))
        else:
            out.append(last[f][j, start - split : end - split].reshape(rows * half, c))
    return jnp.concatenate(out, 1)


def sum_taps(w, u, i):
    s = w[i, 0].astype(F32) + w[i, 2].astype(F32)
    h = w[i, 1].astype(F32)
    u[0, i] = (s + h).astype(BF)
    u[1, i] = (s - h).astype(BF)


def summed_kernels_body(w, u):
    def tap(i, _):
        sum_taps(w, u, i)
        return 0

    lax.fori_loop(0, w.shape[0], tap, 0)


def first_kernels_body(w, w_in, cache_one, cache_two, u, w_big, placed_one, placed_two):
    summed_kernels_body(w, u)

    @pl.when(lax.axis_index("tm") == 0)
    def _():
        place = places(cache_one.shape[2], 1, True)
        for source, placed in ((cache_one, placed_one), (cache_two, placed_two)):
            for f in range(source.shape[0]):
                for r in range(source.shape[1]):
                    placed[f, r] = dot(place, source[f, r]).astype(BF)

    c = w_in.shape[1]
    chan = w_in.shape[0] // 27
    slot = 4 * chan
    w_big[...] = jnp.zeros_like(w_big)
    for dt in range(3):
        for dy in range(3):
            taps = w_in[(3 * dt + dy) * 3 * chan : (3 * dt + dy + 1) * 3 * chan]
            for k in range(2):
                start = (4 * dt + dy + k) * slot
                w_big[start : start + 3 * chan, k * c : (k + 1) * c] = taps


def first_kernels(w, w_in, cache_one, cache_two):
    taps, _, c, o = w.shape
    chan = w_in.shape[0] // 27
    return pl.pallas_call(
        first_kernels_body,
        in_specs=in_vmem(4),
        out_specs=in_vmem(4),
        out_shape=[
            jax.ShapeDtypeStruct((2, taps, c, o), BF),
            jax.ShapeDtypeStruct((48 * chan, 2 * c), BF),
            jax.ShapeDtypeStruct(cache_one.shape, BF),
            jax.ShapeDtypeStruct(cache_two.shape, BF),
        ],
        compiler_params=limit(16),
        name="first_kernels",
        cost_estimate=pl.CostEstimate(flops=6 * taps * c * o, bytes_accessed=10 * taps * c * o, transcendentals=0),
    )(w, w_in, cache_one, cache_two)


def summed_kernels(w):
    taps, _, c, o = w.shape
    return pl.pallas_call(
        summed_kernels_body,
        in_specs=in_vmem(1),
        out_specs=in_vmem(1)[0],
        out_shape=jax.ShapeDtypeStruct((2, taps, c, o), BF),
        compiler_params=limit(16),
        name="summed_kernels",
        cost_estimate=pl.CostEstimate(flops=6 * taps * c * o, bytes_accessed=10 * taps * c * o, transcendentals=0),
    )(w)


def border_rows_body(chan, both, prev1, prev2, one, two, to_dn, to_up):
    size = prev1.shape[0]
    own, cache = both.at[0:size], both.at[size : 2 * size]
    tm = lax.axis_index("tm")
    one[...] = jnp.where(tm == 0, cache[...], prev1[...])
    two[...] = jnp.where(tm == 1, cache[...], prev2[...])
    frame = own.shape[0] // 2
    for f, src in enumerate((two, two, one, one, own, own)):
        at = (f % 2) * frame
        to_dn[f * 3 * chan : (f + 1) * 3 * chan] = src[at + frame - 3 * chan : at + frame]
        to_up[f * 3 * chan : (f + 1) * 3 * chan] = src[at : at + 3 * chan]


def border_rows(chan, both, prev1, prev2):
    same = jax.ShapeDtypeStruct(prev1.shape, BF)
    edge = jax.ShapeDtypeStruct((18 * chan, prev1.shape[1]), BF)
    return pl.pallas_call(
        functools.partial(border_rows_body, chan),
        in_specs=in_vmem(3),
        out_specs=in_vmem(4),
        out_shape=[same, same, edge, edge],
        compiler_params=limit(4),
        name="border_rows",
        cost_estimate=pl.CostEstimate(flops=6_000_000_000, bytes_accessed=400_000, transcendentals=0),
    )(both, prev1, prev2)


def finish_norm(tiles, acc, b_one, gain_two, n2_ref, t, r, at):
    half = n2_ref.shape[2] // 2
    rows = pl.ds(r * half, half)
    m = [acc[j, t, rows] for j in range(4)]
    rows_here = lax.axis_index("tile")
    at_row = rows_here * (tiles[1] // tiles[0]) + at + r - 1
    keep = jnp.logical_and(at_row >= 0, at_row < tiles[1])
    gain = jnp.where(keep, 0.5 * gain_two[...], 0.0)
    even = m[0] + m[1] + m[2] + b_one[...]
    odd = m[1] - m[2] - m[3] + b_one[...]
    n2_ref[t, r, 0:half] = silu_of_twice(rms(even, gain)).astype(BF)
    n2_ref[t, r, half:] = silu_of_twice(rms(odd, gain)).astype(BF)


def conv_normed(tiles, patches, w, acc, b_one, gain_two, n2_ref, at, beside_last, beside_pairs):
    rows = n2_ref.shape[1]

    def middle(j):
        return lambda: jnp.concatenate([patches(1, j), patches(2, j)], 1)

    def finish(t):
        return [
            do(finish_norm, tiles, acc, b_one, gain_two, n2_ref, t, r, at) for r in range(rows)
        ]

    weave(
        [single(acc, w, j, 1, 2, do(patches, 3, j), False) for j in range(4)],
        beside_last,
    )
    pairs = []
    for j in range(4):
        pairs += pair_pieces(acc, w, j, ((1, 0), (2, 1)), middle(j), True)
    weave(pairs, beside_pairs)
    weave([single(acc, w, j, 0, 0, do(patches, 0, j)) for j in range(4)], finish(1))
    weave([lambda: None], finish(0))


def normed_row(tiles, gain_one, hs, f, r):
    tile = lax.axis_index("tile")
    width, c = hs.shape[1] // 4, hs.shape[2] // 2
    rows = tiles[1] // tiles[0]
    p, k = r // 2, r % 2
    h0 = hs[p, f * width : (f + 1) * width, k * c : (k + 1) * c]
    at_row = tile * rows + r - 2
    keep = jnp.logical_and(at_row >= 0, at_row < tiles[1])
    gain = jnp.where(keep, 0.5 * gain_one[...], 0.0)
    return h0, silu_of_twice(rms(h0.astype(F32), gain))


def projection_body(
    tiles,
    both, prev1, prev2, up, dn, w_big, b_in, gain_one,
    hs, v2, v3, h0_ref,
    lats, g,
):
    own = both.at[0 : prev1.shape[0]]
    v = (None, None, v2, v3)
    width = own.shape[-1]
    c = w_big.shape[1] // 2
    chan = w_big.shape[0] // 48
    rows = own.shape[0] // (2 * chan)
    rows1 = rows + 4
    slot = 4 * chan

    empty = jnp.zeros((6, chan, width), BF)
    for r in range(rows + 6):
        lats[:, (r + 1) * slot - chan : (r + 1) * slot] = empty
    place = jnp.concatenate([places(width, dx, False) for dx in range(3)], 1)

    def lay(block, f0, r0, count):
        moved = dot(block, place).astype(BF)
        for i in range(block.shape[0] // chan):
            f, r = f0 + i // count, r0 + i % count
            for dx in range(3):
                lats[f, r * slot + dx * chan : r * slot + (dx + 1) * chan] = moved[
                    i * chan : (i + 1) * chan, dx * width : (dx + 1) * width
                ]

    lay(up[...], 0, 0, 3)
    lay(prev2[...], 0, 3, rows)
    lay(prev1[...], 2, 3, rows)
    lay(own[...], 4, 3, rows)
    lay(dn[...], 0, 3 + rows, 3)
    eye = jnp.where(
        lax.broadcasted_iota(jnp.int32, (width, width), 0)
        == lax.broadcasted_iota(jnp.int32, (width, width), 1),
        1.0,
        0.0,
    ).astype(BF)
    for f in range(6):
        g[f * width : (f + 1) * width] = lax.dot_general(
            eye, lats[f], (((1,), (1,)), ((), ())), preferred_element_type=F32
        ).astype(BF)

    bias = jnp.concatenate([b_in[...], b_in[...]], 1)

    columns = 2 * c // 3

    def project(p):
        def piece(k):
            def product():
                patches = jnp.concatenate(
                    [
                        g[dt * width : (dt + 4) * width, 2 * p * slot : (2 * p + 4) * slot]
                        for dt in range(3)
                    ],
                    1,
                )
                here = slice(k * columns, (k + 1) * columns)
                hs[p, :, here] = (dot(patches, w_big[:, here]) + bias[:, here]).astype(BF)

            return product

        return [piece(k) for k in range(3)]

    def normed(f, r):
        h0, n1 = normed_row(tiles, gain_one, hs, f, r)
        if 2 <= r < 2 + rows:
            h0_ref[f - 2, r - 2] = h0
        put(v, f, r, n1)

    def units(p):
        return [do(normed, f, 2 * p + k) for k in range(2) for f in (2, 3)]

    pairs = rows1 // 2
    weave(project(0), [])
    for p in range(pairs):
        weave(project(p + 1) if p + 1 < pairs else [lambda: None], units(p))


def place_border(border, first, count, cached):
    @pl.when(lax.axis_index("tm") == 0)
    def _():
        place = places(border.shape[2], 1, True)
        for f in range(2):
            for i in range(count):
                cached[f, i] = dot(place, border[f, first + i]).astype(BF)


def earlier_units(tiles, gain_one, hs, v, source, f, first, count):
    at_start = lax.axis_index("tm") == 0

    def normed(i):
        _, n1 = normed_row(tiles, gain_one, hs, f, first + i)
        put(v, f, i, jnp.where(at_start, source(f, first + i).astype(F32), n1))

    return [do(normed, i) for i in range(count)]


def first_part_body(
    tiles, hs, v2, v3, placed, cache_up, gain_one, w, u, b_one, gain_two,
    n2_ref, v0, v1,
    cached, acc,
):
    v = (v0, v1, v2, v3)
    rows = n2_ref.shape[1]
    needed = rows + 2
    place_border(cache_up, 0, 2, cached)

    def source(f, r):
        return cached[f, r] if r < 2 else placed[f, r - 2]

    def units(f):
        return earlier_units(tiles, gain_one, hs, v, source, f, 0, needed)

    conv_normed(
        tiles, lambda f, j: rows_of(v, f, j, 0, rows), plain_and_sums(w, u), acc, b_one,
        gain_two, n2_ref, 0, units(1), units(0),
    )


def second_part_body(
    tiles, hs, v0, v1, v2, v3, placed, cache_dn, gain_one, w, u, b_one, gain_two,
    n2_ref, cached, late, acc,
):
    rows = n2_ref.shape[1]
    there = v0.shape[1]
    early, late, own = (v0, v1), (late.at[0], late.at[1]), (None, None, v2, v3)
    here = placed.shape[1] + 2
    place_border(cache_dn, 0, 2, cached)

    def source(f, r):
        return placed[f, r - 2] if r < here else cached[f, r - here]

    def patches(f, j):
        if f < 2:
            return rows_joined(early, late, f, j, rows, rows)
        return rows_of(own, f, j, rows, rows)

    def units(f):
        return earlier_units(tiles, gain_one, hs, late, source, f, there, rows)

    conv_normed(
        tiles, patches, plain_and_sums(w, u), acc, b_one, gain_two, n2_ref, rows,
        units(1), units(0),
    )


def split_earlier(v, f, earlier, source, first):
    at_start = lax.axis_index("tm") == 0

    def split(r):
        row = jnp.where(at_start, source(f, first + r).astype(F32), earlier[f, r].astype(F32))
        put(v, f, r, row)

    return [do(split, r) for r in range(earlier.shape[1])]


def halves(first, second):
    return [(first, r) for r in range(first.shape[1])] + [(second, r) for r in range(second.shape[1])]


def own_frames_body(
    n2a, n2b, earlier, placed, cache_up, w, u, h0, b_two,
    part_ref, ve0, ve1,
    cached, v, acc,
):
    width, c = n2a.shape[2:]
    half = width // 2
    rows = part_ref.shape[1]
    source = halves(n2a, n2b)
    v = (v.at[0], v.at[1])
    place_border(cache_up, 2, 1, cached)

    def cache_row(f, r):
        return cached[f, 0] if r < 1 else placed[f, r - 1]

    def split(f):
        return [
            do(lambda r, ref, at: put(v, f, r, ref[f, at].astype(F32)), r, ref, at)
            for r, (ref, at) in enumerate(source)
        ]

    def finish(t, r):
        m = [acc[j, t, r * half : (r + 1) * half] for j in range(4)]
        even = m[0] + m[1] + m[2] + b_two[...]
        odd = m[1] - m[2] - m[3] + b_two[...]
        part_ref[t, r, 0:half] = even + h0[t, r, 0:half].astype(F32)
        part_ref[t, r, half:] = odd + h0[t, r, half:].astype(F32)

    kernel = plain_and_sums(w, u)

    def pair(j):
        return pair_pieces(acc, kernel, j, ((2, 1),), do(rows_of, v, 0, j, 0, rows))

    def other(j):
        return single(acc, kernel, j, 1, 2, do(rows_of, v, 1, j, 0, rows))

    ve = (ve0, ve1)
    weave([lambda: None], split(0))
    weave(pair(0) + pair(1), split(1))
    weave(
        pair(2) + pair(3),
        split_earlier(ve, 0, earlier, cache_row, 0) + split_earlier(ve, 1, earlier, cache_row, 0),
    )
    weave([other(j) for j in range(4)], [do(finish, 0, r) for r in range(rows)])
    weave([lambda: None], [do(finish, 1, r) for r in range(rows)])


def earlier_frames_body(
    ve0, ve1, earlier, placed, cache_dn, w, u, part, out_ref, cached, late, acc, columns
):
    width, c = earlier.shape[2:]
    half = width // 2
    rows = out_ref.shape[1]
    kernel = plain_and_sums(w, u)
    first = (ve0, ve1)
    late = (late.at[0], late.at[1])
    place_border(cache_dn, 2, 1, cached)
    there = ve0.shape[1]

    def cache_row(f, r):
        return placed[f, r - 1] if r < 1 + rows else cached[f, 0]


    def finish(t, r):
        m = [acc[j, t, r * half : (r + 1) * half] for j in range(4)]
        even = part[t, r, 0:half] + m[0] + m[1] + m[2]
        odd = part[t, r, half:] + m[1] - m[2] - m[3]
        for k in range(c // 128):
            lanes = slice(k * 128, (k + 1) * 128)
            row = columns.at[(t * rows + r) * (c // 128) + k]
            row[pl.ds(0, half, stride=2)] = even[:, lanes]
            row[pl.ds(1, half, stride=2)] = odd[:, lanes]
            out_ref[t, r, :, lanes] = row[...].astype(BF)

    weave([lambda: None], split_earlier(late, 1, earlier, cache_row, there))
    pairs = []
    for j in range(4):
        pairs += pair_pieces(acc, kernel, j, ((1, 0),), do(rows_joined, first, late, 1, j, 0, rows))
    weave(pairs, split_earlier(late, 0, earlier, cache_row, there))
    weave(
        [single(acc, kernel, j, 0, 0, do(rows_joined, first, late, 0, j, 0, rows)) for j in range(4)],
        [do(finish, 1, r) for r in range(rows)],
    )
    weave([lambda: None], [do(finish, 0, r) for r in range(rows)])


def on_device(
    latent, cache_lat, cache_one, cache_two, w_in, b_in, gain_one, w_one, b_one, gain_two, w_two, b_two
):
    frames, rows, width, chan = latent.shape
    c = w_in.shape[-1]
    half = width // 2
    part_rows = (rows + 2) // 2
    tiles = (lax.axis_size("tile"), rows * lax.axis_size("tile"))

    def flat(x):
        return x.reshape(-1, width)

    def row(x):
        return x.reshape(1, c)

    def cost(gflop):
        return pl.CostEstimate(flops=int(gflop * 1e9), bytes_accessed=int(gflop * 1e6), transcendentals=0)

    own = flat(jnp.swapaxes(latent, 2, 3))
    prev1 = shifted(own, "tm", 1)
    prev2 = shifted(own, "tm", 2)
    own_and_cache = jnp.concatenate([own, flat(jnp.swapaxes(cache_lat, 2, 3))], 0)
    prev1, prev2, to_dn, to_up = border_rows(chan, own_and_cache, prev1, prev2)
    up = shifted(to_dn, "tile", 1)
    dn = shifted(to_up, "tile", -1)
    caches = jnp.concatenate([cache_one[:, rows - 2 :], cache_two[:, rows - 1 :]], 1)
    cache_up = first_frames_only(caches, 1)
    caches = jnp.concatenate([cache_one[:, :2], cache_two[:, :1]], 1)
    cache_dn = first_frames_only(caches, -1)

    normed_part = jax.ShapeDtypeStruct((2, part_rows, width, c), BF)
    w1 = w_one.reshape(9, 3, c, c)
    w2 = w_two.reshape(9, 3, c, c)
    u1, w_big, placed_one, placed_two = first_kernels(
        w1, w_in.reshape(-1, c), cache_one, cache_two
    )
    u2 = summed_kernels(w2)
    filtered = jax.ShapeDtypeStruct((4, rows + 4, half, c), BF)
    hs, *v_own, h0 = pl.pallas_call(
        functools.partial(projection_body, tiles),
        out_shape=[
            jax.ShapeDtypeStruct(((rows + 4) // 2, 4 * width, 2 * c), BF),
            filtered,
            filtered,
            jax.ShapeDtypeStruct((2, rows, width, c), BF),
        ],
        in_specs=in_vmem(8),
        out_specs=in_vmem(4),
        scratch_shapes=[
            VMEM((6, (rows + 6) * 4 * chan, width), BF),
            VMEM((6 * width, (rows + 6) * 4 * chan), BF),
        ],
        compiler_params=limit(16),
        name="projection",
        cost_estimate=cost(6),
    )(own_and_cache, prev1, prev2, up, dn, w_big, row(b_in), row(gain_one))
    n2a, *v_earlier = pl.pallas_call(
        functools.partial(first_part_body, tiles),
        out_shape=[normed_part, *[jax.ShapeDtypeStruct((4, part_rows + 2, half, c), BF)] * 2],
        in_specs=in_vmem(10),
        out_specs=in_vmem(3),
        scratch_shapes=[
            VMEM((2, 2, width, c), BF),
            VMEM((4, 2, part_rows * half, c), F32),
        ],
        compiler_params=limit(20),
        name="first_part",
        cost_estimate=cost(8),
    )(
        hs, *v_own, placed_one, cache_up, row(gain_one),
        w1, u1, row(b_one), row(gain_two),
    )
    earlier_a = shifted(n2a, "tm", 1)
    n2b = pl.pallas_call(
        functools.partial(second_part_body, tiles),
        out_shape=normed_part,
        in_specs=in_vmem(12),
        out_specs=in_vmem(1)[0],
        scratch_shapes=[
            VMEM((2, 2, width, c), BF),
            VMEM((2, 4, part_rows, half, c), BF),
            VMEM((4, 2, part_rows * half, c), F32),
        ],
        compiler_params=limit(20),
        name="second_part",
        cost_estimate=cost(0.2),
    )(
        hs, *v_earlier, *v_own, placed_one, cache_dn, row(gain_one),
        w1, u1, row(b_one), row(gain_two),
    )
    earlier_b = shifted(n2b, "tm", 1)
    filtered_part = jax.ShapeDtypeStruct((4, part_rows, half, c), BF)
    part, *ve = pl.pallas_call(
        own_frames_body,
        out_shape=[
            jax.ShapeDtypeStruct((2, rows, width, c), F32),
            filtered_part,
            filtered_part,
        ],
        in_specs=in_vmem(9),
        out_specs=in_vmem(3),
        scratch_shapes=[
            VMEM((2, 2, width, c), BF),
            VMEM((2, 4, rows + 2, half, c), BF),
            VMEM((4, 2, rows * half, c), F32),
        ],
        compiler_params=limit(20),
        name="own_frames",
        cost_estimate=cost(4),
    )(n2a, n2b, earlier_a, placed_two, cache_up, w2, u2, h0, row(b_two))
    return pl.pallas_call(
        earlier_frames_body,
        out_shape=jax.ShapeDtypeStruct((2, rows, width, c), BF),
        in_specs=in_vmem(8),
        out_specs=in_vmem(1)[0],
        scratch_shapes=[
            VMEM((2, 2, width, c), BF),
            VMEM((2, 4, part_rows, half, c), BF),
            VMEM((4, 2, rows * half, c), F32),
            VMEM((2 * rows * (c // 128), width, 128), F32),
        ],
        compiler_params=limit(20),
        name="earlier_frames",
        cost_estimate=cost(4),
    )(*ve, earlier_b, placed_two, cache_dn, w2, u2, part)


def solution(mesh):
    return jax.shard_map(
        on_device,
        mesh=mesh,
        in_specs=(
            P("tm", "tile", None, None),
            P(None, "tile", None, None),
            P(None, "tile", None, None),
            P(None, "tile", None, None),
            P(),
            P(),
            P(),
            P(),
            P(),
            P(),
            P(),
            P(),
        ),
        out_specs=P("tm", "tile", None, None),
        check_vma=False,
    )
```

```python
import functools

import jax
import jax.numpy as jnp
from jax import lax
from jax.experimental import pallas as pl
from jax.experimental.pallas import tpu as pltpu
from jax.sharding import PartitionSpec as P

BF = jnp.bfloat16
F32 = jnp.float32
VMEM = pltpu.VMEM


def shifted(x, axis, by):
    count = lax.axis_size(axis)
    return lax.ppermute(x, axis, [(i, i + by) for i in range(count) if 0 <= i + by < count])


def first_frames_only(x, by):
    rows = lax.axis_size("tile")
    return lax.ppermute(
        x, ("tm", "tile"), [(i, i + by) for i in range(rows) if 0 <= i + by < rows]
    )


def column_of(place, width):
    half = width // 2
    return jnp.where(place < half, 2 * place, 2 * (place - half) + 1)


def silu_of_twice(h):
    return h + h * jnp.tanh(h)


def rms(v, gain):
    return v * lax.rsqrt(jnp.mean(v * v, -1, keepdims=True) + 1e-6) * gain


def filtered(even, odd):
    half, c = even.shape
    place = lax.broadcasted_iota(jnp.int32, (8, c), 0)
    odd_before = pltpu.roll(odd, 1, 0)
    odd_before = jnp.concatenate([jnp.where(place == 0, 0.0, odd_before[:8]), odd_before[8:]], 0)
    even_after = pltpu.roll(even, half - 1, 0)
    even_after = jnp.concatenate(
        [even_after[: half - 8], jnp.where(place == 7, 0.0, even_after[half - 8 :])], 0
    )
    odd_before, odd = odd_before.astype(BF), odd.astype(BF)
    even, even_after = even.astype(BF), even_after.astype(BF)
    return odd_before - odd, 0.5 * (even + odd), 0.5 * (odd - even), even - even_after


def dot(a, b):
    return jnp.dot(a, b, preferred_element_type=F32)


def in_vmem(count):
    return [pl.BlockSpec(memory_space=VMEM)] * count


def limit(mib):
    return pltpu.CompilerParams(vmem_limit_bytes=mib << 20)


def places(width, dx, transposed):
    shape = (width, width)
    to = column_of(lax.broadcasted_iota(jnp.int32, shape, 0 if transposed else 1), width)
    at = lax.broadcasted_iota(jnp.int32, shape, 1 if transposed else 0)
    return jnp.where(at == to + (dx - 1), 1.0, 0.0).astype(BF)


def put(v, f, r, row):
    half = row.shape[0] // 2
    parts = filtered(row[:half], row[half:])
    for j in range(4):
        v[f][j, r] = parts[j]


def plain_and_sums(w, u):
    def tap(j, i, columns):
        if j == 0 or j == 3:
            return w[i, 0 if j == 0 else 2, :, columns]
        return u[j - 1, i, :, columns]

    return tap


def taps_of(w, j, dt, columns=slice(None)):
    return jnp.concatenate([w(j, 3 * dt + dy, columns) for dy in range(3)], 0)


def weave(products, vector):
    done = 0
    for n, product in enumerate(products):
        product()
        upto = len(vector) * (n + 1) // len(products)
        for work in vector[done:upto]:
            work()
        done = upto


def pair_pieces(acc, w, j, dts, patches, add=False):
    c = acc.shape[-1]
    n = 2 * c // 3

    def piece(k):
        def product():
            lo, hi = k * n, (k + 1) * n
            kernels = []
            for dt_a, dt_b in dts:
                parts = []
                if lo < c:
                    parts.append(taps_of(w, j, dt_a, slice(lo, min(hi, c))))
                if hi > c:
                    parts.append(taps_of(w, j, dt_b, slice(max(lo, c) - c, hi - c)))
                kernels.append(jnp.concatenate(parts, 1))
            out = dot(patches(), jnp.concatenate(kernels, 0))
            if lo < c:
                acc[j, 0, :, lo : min(hi, c)] = out[:, : min(hi, c) - lo]
            if hi > c:
                here = slice(max(lo, c) - c, hi - c)
                if add:
                    acc[j, 1, :, here] += out[:, max(c - lo, 0) :]
                else:
                    acc[j, 1, :, here] = out[:, max(c - lo, 0) :]

        return product

    return [piece(k) for k in range(3)]


def single(acc, w, j, t, dt, patches, add=True):
    def product():
        out = dot(patches(), taps_of(w, j, dt))
        acc[j, t] = acc[j, t] + out if add else out

    return product


def do(function, *args):
    return lambda: function(*args)


def rows_of(v, f, j, at, rows):
    half, c = v[f].shape[-2:]
    return jnp.concatenate(
        [v[f][j, at + dy : at + dy + rows].reshape(rows * half, c) for dy in range(3)], 1
    )


def rows_joined(first, last, f, j, at, rows):
    half, c = last[f].shape[-2:]
    split = first[f].shape[1]
    out = []
    for dy in range(3):
        start, end = at + dy, at + dy + rows
        if end <= split:
            out.append(first[f][j, start:end].reshape(rows * half, c))
        elif start < split:
            a = first[f][j, start:split].reshape((split - start) * half, c)
            b = last[f][j, 0 : end - split].reshape((end - split) * half, c)
            out.append(jnp.concatenate([a, b], 0))
        else:
            out.append(last[f][j, start - split : end - split].reshape(rows * half, c))
    return jnp.concatenate(out, 1)


def sum_taps(w, u, i):
    s = w[i, 0].astype(F32) + w[i, 2].astype(F32)
    h = w[i, 1].astype(F32)
    u[0, i] = (s + h).astype(BF)
    u[1, i] = (s - h).astype(BF)


def summed_kernels_body(w, u):
    def tap(i, _):
        sum_taps(w, u, i)
        return 0

    lax.fori_loop(0, w.shape[0], tap, 0, unroll=3)


def first_kernels_body(w, w_in, cache_one, cache_two, u, w_big, placed_one, placed_two):
    summed_kernels_body(w, u)

    @pl.when(lax.axis_index("tm") == 0)
    def _():
        place = places(cache_one.shape[2], 1, True)
        for source, placed in ((cache_one, placed_one), (cache_two, placed_two)):
            for f in range(source.shape[0]):
                for r in range(source.shape[1]):
                    placed[f, r] = dot(place, source[f, r]).astype(BF)

    c = w_in.shape[1]
    chan = w_in.shape[0] // 27
    slot = 4 * chan
    w_big[...] = jnp.zeros_like(w_big)
    for dt in range(3):
        for dy in range(3):
            taps = w_in[(3 * dt + dy) * 3 * chan : (3 * dt + dy + 1) * 3 * chan]
            for k in range(2):
                start = (4 * dt + dy + k) * slot
                w_big[start : start + 3 * chan, k * c : (k + 1) * c] = taps


def first_kernels(w, w_in, cache_one, cache_two):
    taps, _, c, o = w.shape
    chan = w_in.shape[0] // 27
    return pl.pallas_call(
        first_kernels_body,
        in_specs=in_vmem(4),
        out_specs=in_vmem(4),
        out_shape=[
            jax.ShapeDtypeStruct((2, taps, c, o), BF),
            jax.ShapeDtypeStruct((48 * chan, 2 * c), BF),
            jax.ShapeDtypeStruct(cache_one.shape, BF),
            jax.ShapeDtypeStruct(cache_two.shape, BF),
        ],
        compiler_params=limit(16),
        name="first_kernels",
        cost_estimate=pl.CostEstimate(flops=6 * taps * c * o, bytes_accessed=10 * taps * c * o, transcendentals=0),
    )(w, w_in, cache_one, cache_two)


def summed_kernels(w):
    taps, _, c, o = w.shape
    return pl.pallas_call(
        summed_kernels_body,
        in_specs=in_vmem(1),
        out_specs=in_vmem(1)[0],
        out_shape=jax.ShapeDtypeStruct((2, taps, c, o), BF),
        compiler_params=limit(16),
        name="summed_kernels",
        cost_estimate=pl.CostEstimate(flops=6 * taps * c * o, bytes_accessed=10 * taps * c * o, transcendentals=0),
    )(w)


def border_rows_body(chan, both, prev1, prev2, one, two, to_dn, to_up):
    size = prev1.shape[0]
    own, cache = both.at[0:size], both.at[size : 2 * size]
    tm = lax.axis_index("tm")
    one[...] = jnp.where(tm == 0, cache[...], prev1[...])
    two[...] = jnp.where(tm == 1, cache[...], prev2[...])
    frame = own.shape[0] // 2
    for f, src in enumerate((two, two, one, one, own, own)):
        at = (f % 2) * frame
        to_dn[f * 3 * chan : (f + 1) * 3 * chan] = src[at + frame - 3 * chan : at + frame]
        to_up[f * 3 * chan : (f + 1) * 3 * chan] = src[at : at + 3 * chan]


def border_rows(chan, both, prev1, prev2):
    same = jax.ShapeDtypeStruct(prev1.shape, BF)
    edge = jax.ShapeDtypeStruct((18 * chan, prev1.shape[1]), BF)
    return pl.pallas_call(
        functools.partial(border_rows_body, chan),
        in_specs=in_vmem(3),
        out_specs=in_vmem(4),
        out_shape=[same, same, edge, edge],
        compiler_params=limit(4),
        name="border_rows",
        cost_estimate=pl.CostEstimate(flops=6_000_000_000, bytes_accessed=400_000, transcendentals=0),
    )(both, prev1, prev2)


def finish_norm(tiles, acc, b_one, gain_two, n2_ref, t, r, at):
    half = n2_ref.shape[2] // 2
    rows = pl.ds(r * half, half)
    m = [acc[j, t, rows] for j in range(4)]
    rows_here = lax.axis_index("tile")
    at_row = rows_here * (tiles[1] // tiles[0]) + at + r - 1
    keep = jnp.logical_and(at_row >= 0, at_row < tiles[1])
    gain = jnp.where(keep, 0.5 * gain_two[...], 0.0)
    even = m[0] + m[1] + m[2] + b_one[...]
    odd = m[1] - m[2] - m[3] + b_one[...]
    n2_ref[t, r, 0:half] = silu_of_twice(rms(even, gain)).astype(BF)
    n2_ref[t, r, half:] = silu_of_twice(rms(odd, gain)).astype(BF)


def conv_normed(tiles, patches, w, acc, b_one, gain_two, n2_ref, at, beside_last, beside_pairs):
    rows = n2_ref.shape[1]

    def middle(j):
        return lambda: jnp.concatenate([patches(1, j), patches(2, j)], 1)

    def finish(t):
        return [
            do(finish_norm, tiles, acc, b_one, gain_two, n2_ref, t, r, at) for r in range(rows)
        ]

    weave(
        [single(acc, w, j, 1, 2, do(patches, 3, j), False) for j in range(4)],
        beside_last,
    )
    pairs = []
    for j in range(4):
        pairs += pair_pieces(acc, w, j, ((1, 0), (2, 1)), middle(j), True)
    weave(pairs, beside_pairs)
    weave([single(acc, w, j, 0, 0, do(patches, 0, j)) for j in range(4)], finish(1))
    weave([lambda: None], finish(0))


def normed_row(tiles, gain_one, hs, f, r):
    tile = lax.axis_index("tile")
    width, c = hs.shape[1] // 4, hs.shape[2] // 2
    rows = tiles[1] // tiles[0]
    p, k = r // 2, r % 2
    h0 = hs[p, f * width : (f + 1) * width, k * c : (k + 1) * c]
    at_row = tile * rows + r - 2
    keep = jnp.logical_and(at_row >= 0, at_row < tiles[1])
    gain = jnp.where(keep, 0.5 * gain_one[...], 0.0)
    return h0, silu_of_twice(rms(h0.astype(F32), gain))


def projection_body(
    tiles,
    both, prev1, prev2, up, dn, w_big, b_in, gain_one,
    hs, v2, v3, h0_ref,
    lats, g,
):
    own = both.at[0 : prev1.shape[0]]
    v = (None, None, v2, v3)
    width = own.shape[-1]
    c = w_big.shape[1] // 2
    chan = w_big.shape[0] // 48
    rows = own.shape[0] // (2 * chan)
    rows1 = rows + 4
    slot = 4 * chan

    empty = jnp.zeros((6, chan, width), BF)
    for r in range(rows + 6):
        lats[:, (r + 1) * slot - chan : (r + 1) * slot] = empty
    place = jnp.concatenate([places(width, dx, False) for dx in range(3)], 1)

    def lay(block, f0, r0, count):
        moved = dot(block, place).astype(BF)
        for i in range(block.shape[0] // chan):
            f, r = f0 + i // count, r0 + i % count
            for dx in range(3):
                lats[f, r * slot + dx * chan : r * slot + (dx + 1) * chan] = moved[
                    i * chan : (i + 1) * chan, dx * width : (dx + 1) * width
                ]

    lay(up[...], 0, 0, 3)
    lay(prev2[...], 0, 3, rows)
    lay(prev1[...], 2, 3, rows)
    lay(own[...], 4, 3, rows)
    lay(dn[...], 0, 3 + rows, 3)
    eye = jnp.where(
        lax.broadcasted_iota(jnp.int32, (width, width), 0)
        == lax.broadcasted_iota(jnp.int32, (width, width), 1),
        1.0,
        0.0,
    ).astype(BF)
    for f in range(6):
        g[f * width : (f + 1) * width] = lax.dot_general(
            eye, lats[f], (((1,), (1,)), ((), ())), preferred_element_type=F32
        ).astype(BF)

    bias = jnp.concatenate([b_in[...], b_in[...]], 1)

    columns = 2 * c // 3

    def project(p):
        def piece(k):
            def product():
                patches = jnp.concatenate(
                    [
                        g[dt * width : (dt + 4) * width, 2 * p * slot : (2 * p + 4) * slot]
                        for dt in range(3)
                    ],
                    1,
                )
                here = slice(k * columns, (k + 1) * columns)
                hs[p, :, here] = (dot(patches, w_big[:, here]) + bias[:, here]).astype(BF)

            return product

        return [piece(k) for k in range(3)]

    def normed(f, r):
        h0, n1 = normed_row(tiles, gain_one, hs, f, r)
        if 2 <= r < 2 + rows:
            h0_ref[f - 2, r - 2] = h0
        put(v, f, r, n1)

    def units(p):
        return [do(normed, f, 2 * p + k) for k in range(2) for f in (2, 3)]

    pairs = rows1 // 2
    weave(project(0), [])
    for p in range(pairs):
        weave(project(p + 1) if p + 1 < pairs else [lambda: None], units(p))


def place_border(border, first, count, cached):
    @pl.when(lax.axis_index("tm") == 0)
    def _():
        place = places(border.shape[2], 1, True)
        for f in range(2):
            for i in range(count):
                cached[f, i] = dot(place, border[f, first + i]).astype(BF)


def earlier_units(tiles, gain_one, hs, v, source, f, first, count):
    at_start = lax.axis_index("tm") == 0

    def normed(i):
        _, n1 = normed_row(tiles, gain_one, hs, f, first + i)
        put(v, f, i, jnp.where(at_start, source(f, first + i).astype(F32), n1))

    return [do(normed, i) for i in range(count)]


def first_part_body(
    tiles, hs, v2, v3, placed, cache_up, gain_one, w, u, b_one, gain_two,
    n2_ref, v0, v1,
    cached, acc,
):
    v = (v0, v1, v2, v3)
    rows = n2_ref.shape[1]
    needed = rows + 2
    place_border(cache_up, 0, 2, cached)

    def source(f, r):
        return cached[f, r] if r < 2 else placed[f, r - 2]

    def units(f):
        return earlier_units(tiles, gain_one, hs, v, source, f, 0, needed)

    conv_normed(
        tiles, lambda f, j: rows_of(v, f, j, 0, rows), plain_and_sums(w, u), acc, b_one,
        gain_two, n2_ref, 0, units(1), units(0),
    )


def second_part_body(
    tiles, hs, v0, v1, v2, v3, placed, cache_dn, gain_one, w, u, b_one, gain_two,
    n2_ref, cached, late, acc,
):
    rows = n2_ref.shape[1]
    there = v0.shape[1]
    early, late, own = (v0, v1), (late.at[0], late.at[1]), (None, None, v2, v3)
    here = placed.shape[1] + 2
    place_border(cache_dn, 0, 2, cached)

    def source(f, r):
        return placed[f, r - 2] if r < here else cached[f, r - here]

    def patches(f, j):
        if f < 2:
            return rows_joined(early, late, f, j, rows, rows)
        return rows_of(own, f, j, rows, rows)

    def units(f):
        return earlier_units(tiles, gain_one, hs, late, source, f, there, rows)

    conv_normed(
        tiles, patches, plain_and_sums(w, u), acc, b_one, gain_two, n2_ref, rows,
        units(1), units(0),
    )


def split_earlier(v, f, earlier, source, first):
    at_start = lax.axis_index("tm") == 0

    def split(r):
        row = jnp.where(at_start, source(f, first + r).astype(F32), earlier[f, r].astype(F32))
        put(v, f, r, row)

    return [do(split, r) for r in range(earlier.shape[1])]


def halves(first, second):
    return [(first, r) for r in range(first.shape[1])] + [(second, r) for r in range(second.shape[1])]


def own_frames_body(
    n2a, n2b, earlier, placed, cache_up, w, u, h0, b_two,
    part_ref, ve0, ve1,
    cached, v, acc,
):
    width, c = n2a.shape[2:]
    half = width // 2
    rows = part_ref.shape[1]
    source = halves(n2a, n2b)
    v = (v.at[0], v.at[1])
    place_border(cache_up, 2, 1, cached)

    def cache_row(f, r):
        return cached[f, 0] if r < 1 else placed[f, r - 1]

    def split(f):
        return [
            do(lambda r, ref, at: put(v, f, r, ref[f, at].astype(F32)), r, ref, at)
            for r, (ref, at) in enumerate(source)
        ]

    def finish(t, r):
        m = [acc[j, t, r * half : (r + 1) * half] for j in range(4)]
        even = m[0] + m[1] + m[2] + b_two[...]
        odd = m[1] - m[2] - m[3] + b_two[...]
        part_ref[t, r, 0:half] = even + h0[t, r, 0:half].astype(F32)
        part_ref[t, r, half:] = odd + h0[t, r, half:].astype(F32)

    kernel = plain_and_sums(w, u)

    def pair(j):
        return pair_pieces(acc, kernel, j, ((2, 1),), do(rows_of, v, 0, j, 0, rows))

    def other(j):
        return single(acc, kernel, j, 1, 2, do(rows_of, v, 1, j, 0, rows))

    ve = (ve0, ve1)
    weave([lambda: None], split(0))
    weave(pair(0) + pair(1), split(1))
    weave(
        pair(2) + pair(3),
        split_earlier(ve, 0, earlier, cache_row, 0) + split_earlier(ve, 1, earlier, cache_row, 0),
    )
    weave([other(j) for j in range(4)], [do(finish, 0, r) for r in range(rows)])
    weave([lambda: None], [do(finish, 1, r) for r in range(rows)])


def earlier_frames_body(
    ve0, ve1, earlier, placed, cache_dn, w, u, part, out_ref, cached, late, acc, columns
):
    width, c = earlier.shape[2:]
    half = width // 2
    rows = out_ref.shape[1]
    kernel = plain_and_sums(w, u)
    first = (ve0, ve1)
    late = (late.at[0], late.at[1])
    place_border(cache_dn, 2, 1, cached)
    there = ve0.shape[1]

    def cache_row(f, r):
        return placed[f, r - 1] if r < 1 + rows else cached[f, 0]


    def finish(t, r):
        m = [acc[j, t, r * half : (r + 1) * half] for j in range(4)]
        even = part[t, r, 0:half] + m[0] + m[1] + m[2]
        odd = part[t, r, half:] + m[1] - m[2] - m[3]
        for k in range(c // 128):
            lanes = slice(k * 128, (k + 1) * 128)
            row = columns.at[(t * rows + r) * (c // 128) + k]
            row[pl.ds(0, half, stride=2)] = even[:, lanes]
            row[pl.ds(1, half, stride=2)] = odd[:, lanes]
            out_ref[t, r, :, lanes] = row[...].astype(BF)

    weave([lambda: None], split_earlier(late, 1, earlier, cache_row, there))
    pairs = []
    for j in range(4):
        pairs += pair_pieces(acc, kernel, j, ((1, 0),), do(rows_joined, first, late, 1, j, 0, rows))
    weave(pairs, split_earlier(late, 0, earlier, cache_row, there))
    weave(
        [single(acc, kernel, j, 0, 0, do(rows_joined, first, late, 0, j, 0, rows)) for j in range(4)],
        [do(finish, 1, r) for r in range(rows)],
    )
    weave([lambda: None], [do(finish, 0, r) for r in range(rows)])


def on_device(
    latent, cache_lat, cache_one, cache_two, w_in, b_in, gain_one, w_one, b_one, gain_two, w_two, b_two
):
    frames, rows, width, chan = latent.shape
    c = w_in.shape[-1]
    half = width // 2
    part_rows = (rows + 2) // 2
    tiles = (lax.axis_size("tile"), rows * lax.axis_size("tile"))

    def flat(x):
        return x.reshape(-1, width)

    def row(x):
        return x.reshape(1, c)

    def cost(gflop):
        return pl.CostEstimate(flops=int(gflop * 1e9), bytes_accessed=int(gflop * 1e6), transcendentals=0)

    own = flat(jnp.swapaxes(latent, 2, 3))
    prev1 = shifted(own, "tm", 1)
    prev2 = shifted(own, "tm", 2)
    own_and_cache = jnp.concatenate([own, flat(jnp.swapaxes(cache_lat, 2, 3))], 0)
    prev1, prev2, to_dn, to_up = border_rows(chan, own_and_cache, prev1, prev2)
    up = shifted(to_dn, "tile", 1)
    dn = shifted(to_up, "tile", -1)
    caches = jnp.concatenate([cache_one[:, rows - 2 :], cache_two[:, rows - 1 :]], 1)
    cache_up = first_frames_only(caches, 1)
    caches = jnp.concatenate([cache_one[:, :2], cache_two[:, :1]], 1)
    cache_dn = first_frames_only(caches, -1)

    normed_part = jax.ShapeDtypeStruct((2, part_rows, width, c), BF)
    w1 = w_one.reshape(9, 3, c, c)
    w2 = w_two.reshape(9, 3, c, c)
    u1, w_big, placed_one, placed_two = first_kernels(
        w1, w_in.reshape(-1, c), cache_one, cache_two
    )
    u2 = summed_kernels(w2)
    filtered = jax.ShapeDtypeStruct((4, rows + 4, half, c), BF)
    hs, *v_own, h0 = pl.pallas_call(
        functools.partial(projection_body, tiles),
        out_shape=[
            jax.ShapeDtypeStruct(((rows + 4) // 2, 4 * width, 2 * c), BF),
            filtered,
            filtered,
            jax.ShapeDtypeStruct((2, rows, width, c), BF),
        ],
        in_specs=in_vmem(8),
        out_specs=in_vmem(4),
        scratch_shapes=[
            VMEM((6, (rows + 6) * 4 * chan, width), BF),
            VMEM((6 * width, (rows + 6) * 4 * chan), BF),
        ],
        compiler_params=limit(16),
        name="projection",
        cost_estimate=cost(6),
    )(own_and_cache, prev1, prev2, up, dn, w_big, row(b_in), row(gain_one))
    n2a, *v_earlier = pl.pallas_call(
        functools.partial(first_part_body, tiles),
        out_shape=[normed_part, *[jax.ShapeDtypeStruct((4, part_rows + 2, half, c), BF)] * 2],
        in_specs=in_vmem(10),
        out_specs=in_vmem(3),
        scratch_shapes=[
            VMEM((2, 2, width, c), BF),
            VMEM((4, 2, part_rows * half, c), F32),
        ],
        compiler_params=limit(20),
        name="first_part",
        cost_estimate=cost(8),
    )(
        hs, *v_own, placed_one, cache_up, row(gain_one),
        w1, u1, row(b_one), row(gain_two),
    )
    earlier_a = shifted(n2a, "tm", 1)
    n2b = pl.pallas_call(
        functools.partial(second_part_body, tiles),
        out_shape=normed_part,
        in_specs=in_vmem(12),
        out_specs=in_vmem(1)[0],
        scratch_shapes=[
            VMEM((2, 2, width, c), BF),
            VMEM((2, 4, part_rows, half, c), BF),
            VMEM((4, 2, part_rows * half, c), F32),
        ],
        compiler_params=limit(20),
        name="second_part",
        cost_estimate=cost(0.2),
    )(
        hs, *v_earlier, *v_own, placed_one, cache_dn, row(gain_one),
        w1, u1, row(b_one), row(gain_two),
    )
    earlier_b = shifted(n2b, "tm", 1)
    filtered_part = jax.ShapeDtypeStruct((4, part_rows, half, c), BF)
    part, *ve = pl.pallas_call(
        own_frames_body,
        out_shape=[
            jax.ShapeDtypeStruct((2, rows, width, c), F32),
            filtered_part,
            filtered_part,
        ],
        in_specs=in_vmem(9),
        out_specs=in_vmem(3),
        scratch_shapes=[
            VMEM((2, 2, width, c), BF),
            VMEM((2, 4, rows + 2, half, c), BF),
            VMEM((4, 2, rows * half, c), F32),
        ],
        compiler_params=limit(20),
        name="own_frames",
        cost_estimate=cost(4),
    )(n2a, n2b, earlier_a, placed_two, cache_up, w2, u2, h0, row(b_two))
    return pl.pallas_call(
        earlier_frames_body,
        out_shape=jax.ShapeDtypeStruct((2, rows, width, c), BF),
        in_specs=in_vmem(8),
        out_specs=in_vmem(1)[0],
        scratch_shapes=[
            VMEM((2, 2, width, c), BF),
            VMEM((2, 4, part_rows, half, c), BF),
            VMEM((4, 2, rows * half, c), F32),
            VMEM((2 * rows * (c // 128), width, 128), F32),
        ],
        compiler_params=limit(20),
        name="earlier_frames",
        cost_estimate=cost(4),
    )(*ve, earlier_b, placed_two, cache_dn, w2, u2, part)


def solution(mesh):
    return jax.shard_map(
        on_device,
        mesh=mesh,
        in_specs=(
            P("tm", "tile", None, None),
            P(None, "tile", None, None),
            P(None, "tile", None, None),
            P(None, "tile", None, None),
            P(),
            P(),
            P(),
            P(),
            P(),
            P(),
            P(),
            P(),
        ),
        out_specs=P("tm", "tile", None, None),
        check_vma=False,
    )
```
